32 devices in a mesh: cluster: 4 (over x, core), shard: 8 (over z, y).
Axes of the slice: x: 2, y: 2, z: 4, core: 2. Of those that a mesh axis runs over, the one named last changes fastest.
Arguments:
- flow_start: float32 [512, 256], P(('cluster', 'shard')), may hold values from 0 to 1
- demand: float32 [512, 256], P(('cluster', 'shard')), may hold values from 0.25 to 2
- utility: float32 [512, 256], P(('cluster', 'shard')), may hold values from 1 to 16
- path_count: int32 [512], P(('cluster', 'shard')), may hold values from 1 to 256, as said below
- cluster_size: int32 [4], P('cluster'), may hold values from 1 to 16, as said below
- incidence: float32 [1024, 256, 128], P(('cluster', 'shard')), may hold values from 0 to 1, as said below
- inc_path: int32 [1024], P(('cluster', 'shard')), may hold values from 0 to 127, as said below
- inc_edge: int32 [1024], P(('cluster', 'shard')), may hold values from 0 to 6
- capacity: float32 [224, 128], P(('cluster', 'shard')), may hold values from 0.25 to 4
- dual_start: float32 [224, 128], P(('cluster', 'shard')), may hold values from 0 to 7
- partner: int32 [4, 3], P('cluster'), may hold values from 0 to 3, as said below
Outputs:
- flows: float32 [512, 256], P(('cluster', 'shard'))
- duals: float32 [224, 128], P(('cluster', 'shard'))
The draws below stay inside these ranges and needn't reach their ends.
Inputs may be any that keep to these rules, and one draw needn't show every extreme that they name: `path_count`: some path block has 256 live paths. `cluster_size`: some cluster has 16. partner[c, k] = q implies partner[q, k] = c; the partners of a cluster are distinct and differ from it. `incidence`: every entry is 0 or 1. Among the 32 incidence blocks of one device, at most 8 have the same value of inc_path // 16, and on every device some value is taken by exactly 8.
All inputs are finite; a program needn't handle non-finite values.
Results may differ from the reference program's by a relative error of at most 0.0001.
Values sent between devices are 32-bit elements; how exact they have to be, the bound alone decides.
No kernel may reach another device: no remote copies, remote signals or barrier semaphores. Data moves between devices by JAX's collectives and lax.ppermute only.
A program may use at most 64 MiB of HBM per device.

```python
import math
import jax
import jax.numpy as jnp
from jax import lax

PATH = 256
EDGE = 128
PB_DEV = 16
NI = 32
EB_DEV = 4
ITERS = 3
KP = 3
NBL = 7
PB_C = 128
PATHBLK = 512
INCBLK = 1024
EDGEBLK = 224
REQ = 8
LOAD_UNIT = 7
NORM_BOUND = 292
N_CLUSTER = 4
N_SHARD = 8


def draw_path_count(key, part):
    key_full, key_ragged = jax.random.split(key)
    full_flag = jax.random.randint(key_full, (PATHBLK,), 0, 2)
    ragged = jax.random.randint(key_ragged, (PATHBLK,), 1, PATH + 1)
    counts = jnp.where(full_flag == 1, PATH, ragged)
    return counts.at[0].set(PATH).astype(jnp.int32)


def draw_cluster_size(key, part):
    key_sizes, key_chosen = jax.random.split(key)
    sizes = jax.random.randint(key_sizes, (N_CLUSTER,), 1, PB_DEV + 1)
    chosen = jax.random.randint(key_chosen, (), 0, N_CLUSTER)
    return sizes.at[chosen].set(PB_DEV).astype(jnp.int32)


def draw_partner(key, part):
    ordering = jax.random.permutation(key, N_CLUSTER).astype(jnp.int32)
    inverse = jnp.argsort(ordering).astype(jnp.int32)
    slot_ids = jnp.arange(1, KP + 1, dtype=jnp.int32)
    return inverse[jnp.bitwise_xor(ordering[:, None], slot_ids[None, :])].astype(jnp.int32)


def draw_incidence(key, part):
    picks = jax.random.randint(key, (INCBLK, PATH, EDGE), 0, 32)
    return (picks == 0).astype(jnp.float32)


def draw_inc_path(key, part):
    base_key = jax.random.fold_in(key, 7001)
    slot_total = N_SHARD * REQ
    slot_ids = jnp.arange(slot_total, dtype=jnp.int32)
    slot_owner = slot_ids // REQ

    def one_device(device):
        device_key = jax.random.fold_in(base_key, device)
        key_chosen, key_rank, key_block, key_order = jax.random.split(device_key, 4)
        chosen = jax.random.randint(key_chosen, (), 0, N_SHARD)
        ranking = jax.random.permutation(key_rank, slot_total).astype(jnp.int32)
        score = jnp.where(slot_owner == chosen, slot_ids, slot_total + ranking)
        order = jnp.argsort(score, stable=True)
        owners = slot_owner[order[:NI]]
        owners = owners[jax.random.permutation(key_order, NI)]
        blocks = jax.random.randint(key_block, (NI,), 0, PB_DEV)
        return (owners * PB_DEV + blocks).astype(jnp.int32)
    devices = jnp.arange(INCBLK // NI, dtype=jnp.int32)
    return jax.vmap(one_device)(devices).reshape(INCBLK).astype(jnp.int32)


def plant(array, rng, least, largest):
    longest = array.shape.index(max(array.shape))
    spots = []
    for shift in (0, 1):
        where = [jax.random.randint(jax.random.fold_in(rng, axis), (), 0, length) for axis, length in enumerate(array.shape)]
        where[longest] = (where[longest] + shift) % array.shape[longest]
        spots.append(tuple(where))
    return array.at[spots[0]].set(least).at[spots[1]].set(largest)


def shard_levels(stream_key, shape, cuts, low, high):
    loudness, own = 1.0, jax.random.fold_in(stream_key, 6)
    for position, parts in cuts:
        steps = jnp.exp(jax.random.uniform(jax.random.fold_in(own, position), (parts,), jnp.float32, low / len(cuts), high / len(cuts)))
        loudness = loudness * jnp.repeat(steps, shape[position] // parts).reshape([-1 if axis == position else 1 for axis in range(len(shape))])
    return loudness


def setup_inputs(seed: int = 0) -> dict:
    seeds = jax.random.split(jax.random.key(seed), 12)
    flow_start = jnp.clip(1.0 * jax.random.uniform(seeds[0], (PATHBLK, PATH), jnp.float32) ** shard_levels(seeds[0], (PATHBLK, PATH), ((0, 32),), -0.2, 0.2), 0.0, 1.0)
    demand = jnp.clip(jnp.exp(math.log(2.0) - 2.0794415 * jax.random.uniform(seeds[1], (PATHBLK, PATH), jnp.float32) ** shard_levels(seeds[1], (PATHBLK, PATH), ((0, 32),), -0.2, 0.2)), 0.25, 2.0)
    utility = jnp.clip(jnp.exp(math.log(16.0) - 2.7725887 * jax.random.uniform(seeds[2], (PATHBLK, PATH), jnp.float32) ** shard_levels(seeds[2], (PATHBLK, PATH), ((0, 32),), -0.2, 0.2)), 1.0, 16.0)
    path_count = draw_path_count(jax.random.fold_in(seeds[11], 71), 0)
    cluster_size = draw_cluster_size(jax.random.fold_in(seeds[11], 71), 0)
    incidence = draw_incidence(jax.random.fold_in(seeds[11], 71), 0)
    inc_path = draw_inc_path(jax.random.fold_in(seeds[11], 71), 0)
    inc_edge = plant(jax.random.randint(seeds[7], (INCBLK,), 0, NBL), jax.random.fold_in(seeds[7], 1), 0, NBL - 1).astype(jnp.int32)
    capacity = jnp.clip(jnp.exp(math.log(4.0) - 2.7725887 * jax.random.uniform(seeds[8], (EDGEBLK, EDGE), jnp.float32) ** shard_levels(seeds[8], (EDGEBLK, EDGE), ((0, 32),), -0.2, 0.2)), 0.25, 4.0)
    dual_start = jnp.clip(7.0 * jax.random.uniform(seeds[9], (EDGEBLK, EDGE), jnp.float32) ** shard_levels(seeds[9], (EDGEBLK, EDGE), ((0, 32),), -0.2, 0.2), 0.0, 7.0)
    partner = draw_partner(jax.random.fold_in(seeds[11], 71), 0)
    return dict(flow_start=flow_start, demand=demand, utility=utility, path_count=path_count, cluster_size=cluster_size, incidence=incidence, inc_path=inc_path, inc_edge=inc_edge, capacity=capacity, dual_start=dual_start, partner=partner)


def twin_blocks(blocks, partner):
    layout = blocks.reshape(N_CLUSTER, N_SHARD, NBL, EDGE)
    border = layout[:, :, EB_DEV:, :]
    slot_ids = jnp.arange(KP, dtype=jnp.int32)
    twin_part = border[partner, :, slot_ids[None, :]]
    return layout, border, jnp.transpose(twin_part, (0, 2, 1, 3))


def rebuild(layout, border_new):
    joined = jnp.concatenate([layout[:, :, :EB_DEV, :], border_new], axis=2)
    return joined.reshape(EDGEBLK, EDGE)


def reference(flow_start, demand, utility, path_count, cluster_size, incidence, inc_path, inc_edge, capacity, dual_start, partner):
    exact_mode = lax.Precision.HIGHEST
    block_ids = jnp.arange(PATHBLK, dtype=jnp.int32)
    cluster_of = block_ids // PB_C
    live_block = (block_ids % PB_DEV) < cluster_size[cluster_of]
    path_ids = jnp.arange(PATH, dtype=jnp.int32)
    live_mask = (live_block[:, None] & (path_ids[None, :] < path_count[:, None])).astype(jnp.float32)
    inc_ids = jnp.arange(INCBLK, dtype=jnp.int32)
    device_of = inc_ids // NI
    path_rows = ((device_of // N_SHARD) * PB_C + inc_path).astype(jnp.int32)
    edge_rows = (device_of * NBL + inc_edge).astype(jnp.int32)
    capacity_unit = float(LOAD_UNIT)
    step_size = 1.0 / (2.0 * NORM_BOUND)

    layout, border, twin_part = twin_blocks(capacity, partner)
    limit = capacity_unit * rebuild(layout, 0.5 * (border + twin_part))
    layout, border, twin_part = twin_blocks(dual_start, partner)
    duals = rebuild(layout, 0.5 * (border + twin_part))

    def total_load(flows_now):
        picked = flows_now[path_rows]
        terms = jnp.einsum("ipe,ip->ie", incidence, picked, precision=exact_mode)
        own_load = jax.ops.segment_sum(terms, edge_rows, num_segments=EDGEBLK)
        layout_now, border_now, twin_now = twin_blocks(own_load, partner)
        return rebuild(layout_now, border_now + twin_now)

    flows = jnp.minimum(jnp.maximum(flow_start, 0.0), demand) * live_mask
    load = total_load(flows)
    split = jnp.minimum(limit, load + duals)
    duals = (duals + load) - split
    for iteration in range(ITERS):
        residual = (load - split) + duals
        back_terms = jnp.einsum("ipe,ie->ip", incidence, residual[edge_rows], precision=exact_mode)
        gradient = jax.ops.segment_sum(back_terms, path_rows, num_segments=PATHBLK)
        flows = jnp.minimum(jnp.maximum(flows - step_size * (gradient - utility), 0.0), demand) * live_mask
        load = total_load(flows)
        split = jnp.minimum(limit, load + duals)
        duals = (duals + load) - split
    return flows, duals
```

```python
import jax
import jax.numpy as jnp
from jax import lax
from jax.experimental import pallas as pl
from jax.experimental.pallas import tpu as pltpu
from jax.sharding import PartitionSpec as P

ITERS = 3
SUB = 8
VMEM = pl.BlockSpec(memory_space=pltpu.VMEM)
SMEM = pl.BlockSpec(memory_space=pltpu.SMEM)


def split3(x):
    high = x.astype(jnp.bfloat16)
    rest = x - high.astype(jnp.float32)
    middle = rest.astype(jnp.bfloat16)
    low = (rest - middle.astype(jnp.float32)).astype(jnp.bfloat16)
    return high, middle, low


def pick_rows(onehot, rows):
    total = None
    for part in split3(rows):
        term = jnp.dot(onehot, part, preferred_element_type=jnp.float32)
        total = term if total is None else total + term
    return total


def prep_kernel(
    start_ref, demand_ref, utility_ref, cap_ref, dual_ref, ids_ref, count_ref, size_ref,
    first_ref, second_ref, border_ref,
):
    blocks, width = start_ref.shape
    edges = cap_ref.shape[1]
    slots = border_ref.shape[0] // 2
    interior = cap_ref.shape[0] - slots
    lanes = lax.broadcasted_iota(jnp.int32, (1, width), 1)
    limits = []
    for j in range(blocks):
        count = jnp.where(j < size_ref[0], count_ref[j], 0)
        limits.append(jnp.where(lanes < count, demand_ref[j : j + 1, :], 0.0))
    limit = jnp.concatenate(limits, axis=0)
    first_ref[:blocks] = jnp.minimum(jnp.maximum(start_ref[...], 0.0), limit)
    ids = ids_ref[...].astype(jnp.float32)
    first_ref[blocks:] = jnp.zeros((SUB, width), jnp.float32)
    first_ref[blocks : blocks + 1, : ids.shape[1]] = ids
    second_ref[:blocks] = limit
    second_ref[blocks:] = utility_ref[...]
    border_ref[:slots] = cap_ref[interior:]
    border_ref[slots:] = dual_ref[interior:]


def load_of(flows, mask, inc_ref):
    count, _, edges = inc_ref.shape
    parts = [p.astype(jnp.float32) for p in split3(flows)]
    total = jnp.zeros((3 * SUB, edges), jnp.float32)
    for i in range(count):
        column = mask[:, i : i + 1]
        rows = jnp.concatenate([p[i : i + 1] * column for p in parts], axis=0)
        total += jnp.dot(rows.astype(jnp.bfloat16), inc_ref[i], preferred_element_type=jnp.float32)
    return total[:SUB] + total[SUB : 2 * SUB] + total[2 * SUB :]


def put_load(load, load_ref, border_ref):
    slots = border_ref.shape[0]
    interior = load_ref.shape[0] - slots
    load_ref[...] = load[: load_ref.shape[0]]
    border_ref[...] = load[interior : interior + slots]


def start_kernel(pieces, *refs):
    ins, (onehot_ref, mask_ref, inc_ref, flows_ref, load_ref, border_ref) = refs[:pieces], refs[pieces:]
    blocks = flows_ref.shape[0] - inc_ref.shape[0]
    group = blocks + SUB
    rows = jnp.concatenate(
        [ref[k : k + blocks] for ref in ins for k in range(0, ref.shape[0], group)], axis=0
    )
    flows = pick_rows(onehot_ref[...], rows)
    flows_ref[...] = flows
    put_load(load_of(flows[: inc_ref.shape[0]], mask_ref[...], inc_ref), load_ref, border_ref)


def pick_kernel(pieces, blocks, *refs):
    ins, (onehot_ref, limit_ref, utility_ref) = refs[:pieces], refs[pieces:]
    for offset, out in ((0, limit_ref), (blocks, utility_ref)):
        rows = jnp.concatenate(
            [
                ref[k : k + blocks]
                for ref in ins
                for k in range(offset, ref.shape[0], 2 * blocks)
            ],
            axis=0,
        )
        out[...] = pick_rows(onehot_ref[...], rows)


def flow_kernel(pieces, step_size, *refs):
    ins = refs[:pieces]
    (same_ref, flows_ref, limit_ref, utility_ref, mask_ref, inc_ref,
     out_ref, load_ref, border_ref) = refs[pieces:]
    terms = jnp.concatenate([ref[...] for ref in ins], axis=0)
    gradient = pick_rows(same_ref[...], terms)
    flows = flows_ref[...] - step_size * (gradient - utility_ref[...])
    flows = jnp.minimum(jnp.maximum(flows, 0.0), limit_ref[...])
    out_ref[...] = flows
    put_load(load_of(flows[: inc_ref.shape[0]], mask_ref[...], inc_ref), load_ref, border_ref)


def twin_of(ins, choice_ref):
    total = None
    for k, ref in enumerate(ins):
        term = jnp.where(choice_ref[k] > 0.5, ref[...], 0.0)
        total = term if total is None else total + term
    return total


def settle(ins, choice_ref, load_ref, limit, duals):
    load = load_ref[...]
    slots = ins[0].shape[0]
    interior = load.shape[0] - slots
    load = jnp.concatenate([load[:interior], load[interior:] + twin_of(ins, choice_ref)], axis=0)
    split = jnp.minimum(limit, load + duals)
    duals = (duals + load) - split
    return (load - split) + duals, duals


def back_terms(residual, mask, inc_ref, out_ref):
    rows = residual.shape[0]
    if rows < SUB:
        residual = jnp.concatenate(
            [residual, jnp.zeros((SUB - rows, residual.shape[1]), jnp.float32)], axis=0
        )
    parts = [p.astype(jnp.float32) for p in split3(residual)]
    left = jnp.concatenate(parts, axis=0).astype(jnp.bfloat16)
    for i in range(inc_ref.shape[0]):
        got = lax.dot_general(
            left, inc_ref[i], (((1,), (1,)), ((), ())), preferred_element_type=jnp.float32
        )
        got = got[:SUB] + got[SUB : 2 * SUB] + got[2 * SUB :]
        out_ref[i : i + 1, :] = jnp.sum(got * mask[:, i : i + 1], axis=0, keepdims=True)


def first_dual_kernel(others, unit, *refs):
    ins, starts = refs[:others], refs[others : 2 * others]
    (choice_ref, load_ref, cap_ref, dual_ref, mask_ref, inc_ref,
     limit_ref, out_ref, terms_ref) = refs[2 * others :]
    slots = ins[0].shape[0]
    interior = load_ref.shape[0] - slots
    cap_in = [r.at[:slots] for r in starts]
    dual_in = [r.at[slots:] for r in starts]

    def shared(ref, twins):
        mean = 0.5 * (ref[interior:] + twin_of(twins, choice_ref))
        return jnp.concatenate([ref[:interior], mean], axis=0)

    limit = unit * shared(cap_ref, cap_in)
    limit_ref[...] = limit
    residual, duals = settle(ins, choice_ref, load_ref, limit, shared(dual_ref, dual_in))
    out_ref[...] = duals
    back_terms(residual, mask_ref[...], inc_ref, terms_ref)


def dual_kernel(others, *refs):
    ins = refs[:others]
    (choice_ref, load_ref, limit_ref, dual_ref, mask_ref, inc_ref,
     out_ref, terms_ref) = refs[others:]
    residual, duals = settle(ins, choice_ref, load_ref, limit_ref[...], dual_ref[...])
    out_ref[...] = duals
    back_terms(residual, mask_ref[...], inc_ref, terms_ref)


def last_dual_kernel(others, *refs):
    ins = refs[:others]
    choice_ref, load_ref, limit_ref, dual_ref, out_ref = refs[others:]
    out_ref[...] = settle(ins, choice_ref, load_ref, limit_ref[...], dual_ref[...])[1]


def kernel_call(kernel, name, outs, operands, scalars=0, flops=0):
    shapes = tuple(jax.ShapeDtypeStruct(shape, jnp.float32) for shape in outs)
    size = sum(x.size * x.dtype.itemsize for x in operands)
    return pl.pallas_call(
        kernel,
        out_shape=shapes,
        in_specs=[VMEM] * (len(operands) - scalars) + [SMEM] * scalars,
        out_specs=tuple(VMEM for _ in outs),
        compiler_params=pltpu.CompilerParams(vmem_limit_bytes=16 * 1024 * 1024),
        cost_estimate=pl.CostEstimate(flops=flops, bytes_accessed=size, transcendentals=0),
        name=name,
    )(*operands)


def body(
    flow_start,
    demand,
    utility,
    path_count,
    cluster_size,
    incidence,
    inc_path,
    inc_edge,
    capacity,
    dual_start,
    partner,
):
    blocks, width = flow_start.shape
    incs = incidence.shape[0]
    edges = incidence.shape[2]
    locals_ = capacity.shape[0]
    slots = partner.shape[1]
    clusters, devices = lax.axis_size("cluster"), lax.axis_size("shard")
    cluster, shard = lax.axis_index("cluster"), lax.axis_index("shard")
    rows = incs + blocks
    norm_bound = max(2, incs * incs * width * edges // (1024 * locals_ * blocks))
    unit = float(max(1, incs * width // (160 * locals_)))
    step_size = 1.0 / (2.0 * norm_bound)
    bits = devices.bit_length() - 1
    assert devices == 1 << bits and clusters & (clusters - 1) == 0
    stages = [1] * (bits % 2) + [2] * (bits // 2)

    def share(x):
        pieces, shift = [x], 0
        for step in stages:
            now = pieces[0] if len(pieces) == 1 else jnp.concatenate(pieces, axis=0)
            pieces = [now]
            for k in range(1, 1 << step):
                pairs = [(i, i ^ (k << shift)) for i in range(devices)]
                pieces.append(lax.ppermute(now, "shard", pairs))
            shift += step
        return pieces

    def trade(x):
        return [
            lax.ppermute(x, "cluster", [(i, i ^ k) for i in range(clusters)])
            for k in range(1, clusters)
        ]

    inc = incidence.astype(jnp.bfloat16)
    first, second, border = kernel_call(
        prep_kernel,
        "prepare",
        [(blocks + SUB, width), (2 * blocks, width), (2 * slots, edges)],
        [flow_start, demand, utility, capacity, dual_start, inc_path[None, :], path_count, cluster_size],
        scalars=2,
    )
    own_rows = jnp.arange(blocks, dtype=jnp.int32)
    place = jnp.concatenate([((inc_path // blocks) ^ shard) * blocks + inc_path % blocks, own_rows])
    onehot = (place[:, None] == jnp.arange(blocks * devices, dtype=jnp.int32)).astype(jnp.bfloat16)
    mask = (jnp.arange(SUB, dtype=jnp.int32)[:, None] == inc_edge[None, :]).astype(jnp.float32)
    choice = (partner[0][None, :] == (cluster ^ jnp.arange(1, clusters, dtype=jnp.int32))[:, None])
    choice = jnp.broadcast_to(choice.astype(jnp.float32)[:, :, None], (clusters - 1, slots, edges))

    firsts = share(first)
    starts = trade(border)
    seconds = share(second)
    ids = jnp.concatenate([p.reshape(-1, blocks + SUB, width)[:, blocks, :incs] for p in firsts], axis=0)
    names = jnp.concatenate([inc_path, shard * blocks + own_rows]).astype(jnp.float32)
    same = (names[:, None] == ids.reshape(1, -1)).astype(jnp.bfloat16)

    pieces, others = len(firsts), clusters - 1
    flops = 2 * incs * width * edges * SUB
    load_shapes = [(rows, width), (locals_, edges), (slots, edges)]
    flows, load, out = kernel_call(
        lambda *refs: start_kernel(pieces, *refs), "first_load", load_shapes,
        [*firsts, onehot, mask, inc], flops=flops,
    )
    limits, utilities = kernel_call(
        lambda *refs: pick_kernel(pieces, blocks, *refs), "pick", [(rows, width)] * 2,
        [*seconds, onehot],
    )
    dual_shape, term_shape = (locals_, edges), (incs, width)
    limit, duals, terms = kernel_call(
        lambda *refs: first_dual_kernel(others, unit, *refs), "first_duals",
        [dual_shape, dual_shape, term_shape],
        [*trade(out), *starts, choice, load, capacity, dual_start, mask, inc], flops=flops,
    )
    for iteration in range(ITERS):
        flows, load, out = kernel_call(
            lambda *refs: flow_kernel(pieces, step_size, *refs), "flows", load_shapes,
            [*share(terms), same, flows, limits, utilities, mask, inc], flops=flops,
        )
        operands = [*trade(out), choice, load, limit, duals]
        if iteration < ITERS - 1:
            duals, terms = kernel_call(
                lambda *refs: dual_kernel(others, *refs), "duals", [dual_shape, term_shape],
                [*operands, mask, inc], flops=flops,
            )
    (duals,) = kernel_call(
        lambda *refs: last_dual_kernel(others, *refs), "last_duals", [dual_shape], operands
    )
    return flows[incs:], duals


def solution(mesh):
    whole = P(("cluster", "shard"))
    wide = P(("cluster", "shard"), None)
    return jax.shard_map(
        body,
        mesh=mesh,
        in_specs=(
            wide, wide, wide, whole, P("cluster"), P(("cluster", "shard"), None, None),
            whole, whole, wide, wide, P("cluster", None),
        ),
        out_specs=(wide, wide),
        check_vma=False,
    )
```

```python
import jax
import jax.numpy as jnp
from jax import lax
from jax.experimental import pallas as pl
from jax.experimental.pallas import tpu as pltpu
from jax.sharding import PartitionSpec as P

ITERS = 3
SUB = 8
VMEM = pl.BlockSpec(memory_space=pltpu.VMEM)


def split3(x):
    high = x.astype(jnp.bfloat16)
    rest = x - high.astype(jnp.float32)
    middle = rest.astype(jnp.bfloat16)
    low = (rest - middle.astype(jnp.float32)).astype(jnp.bfloat16)
    return high, middle, low


def pick_rows(onehot, rows):
    total = None
    for part in split3(rows):
        term = jnp.dot(onehot, part, preferred_element_type=jnp.float32)
        total = term if total is None else total + term
    return total


def column_of(row):
    n = row.shape[1]
    down = lax.broadcasted_iota(jnp.int32, (n, n), 0)
    along = lax.broadcasted_iota(jnp.int32, (n, n), 1)
    return jnp.sum(jnp.where(down == along, row, 0.0), axis=1, keepdims=True)


def prep_kernel(
    start_hbm, demand_hbm, utility_hbm, cap_hbm, dual_hbm, path_hbm, edge_hbm, count_hbm, size_hbm, partner_hbm,
    first_ref, second_ref, border_ref, onehot_ref, mask_ref, choice_ref,
    start_ref, demand_ref, cap_ref, dual_ref, path_ref, edge_ref, count_ref, size_ref, partner_ref, sems,
):
    blocks, width = start_ref.shape
    slots = border_ref.shape[0] // 2
    interior = cap_ref.shape[0] - slots
    incs = path_ref.shape[1]
    copies = [
        pltpu.make_async_copy(source, target, sems.at[k])
        for k, (source, target) in enumerate(
            [
                (start_hbm, start_ref),
                (demand_hbm, demand_ref),
                (utility_hbm, second_ref.at[blocks : 2 * blocks]),
                (cap_hbm, cap_ref),
                (dual_hbm, dual_ref),
                (path_hbm, path_ref),
                (edge_hbm, edge_ref),
                (count_hbm, count_ref),
                (size_hbm, size_ref),
                (partner_hbm, partner_ref),
            ]
        )
    ]
    for copy in copies:
        copy.start()
    cluster, shard = lax.axis_index("cluster"), lax.axis_index("shard")
    for copy in copies:
        copy.wait()
    lanes = lax.broadcasted_iota(jnp.int32, (1, width), 1)
    limits = []
    for j in range(blocks):
        count = jnp.where(j < size_ref[0], count_ref[j], 0)
        limits.append(jnp.where(lanes < count, demand_ref[j : j + 1, :], 0.0))
    limit = jnp.concatenate(limits, axis=0)
    first_ref[...] = jnp.minimum(jnp.maximum(start_ref[...], 0.0), limit)
    second_ref[:blocks] = limit
    names = path_ref[...]
    second_ref[2 * blocks :] = jnp.zeros((SUB, width), jnp.float32)
    second_ref[2 * blocks : 2 * blocks + 1, :incs] = names.astype(jnp.float32)
    border_ref[:slots] = cap_ref[interior:]
    border_ref[slots:] = dual_ref[interior:]
    place = jnp.bitwise_xor(names // blocks, shard) * blocks + names % blocks
    total = onehot_ref.shape[1]
    along = lax.broadcasted_iota(jnp.int32, (incs, total), 1).astype(jnp.float32)
    picked = jnp.where(along == column_of(place.astype(jnp.float32)), 1.0, 0.0)
    down = lax.broadcasted_iota(jnp.int32, (blocks, total), 0)
    own = jnp.where(down == lax.broadcasted_iota(jnp.int32, (blocks, total), 1), 1.0, 0.0)
    onehot_ref[...] = jnp.concatenate([picked, own], axis=0).astype(jnp.bfloat16)
    edge = lax.broadcasted_iota(jnp.int32, mask_ref.shape, 0)
    mask_ref[...] = jnp.where(edge == edge_ref[...], 1.0, 0.0)
    for k in range(choice_ref.shape[0]):
        for j in range(slots):
            chosen = jnp.where(partner_ref[0, j] == jnp.bitwise_xor(cluster, k + 1), 1.0, 0.0)
            choice_ref[k, j : j + 1, :] = jnp.full((1, choice_ref.shape[2]), chosen, jnp.float32)


def cast_kernel(inc_ref, out_ref):
    out_ref[...] = inc_ref[...].astype(jnp.bfloat16)


def turn_kernel(inc_ref, out_ref):
    for i in range(inc_ref.shape[0]):
        out_ref[i] = inc_ref[i].T


def load_of(flows, mask, inc_ref):
    count, _, edges = inc_ref.shape
    parts = [p.astype(jnp.float32) for p in split3(flows)]
    total = jnp.zeros((3 * SUB, edges), jnp.float32)
    for i in range(count):
        column = mask[:, i : i + 1]
        rows = jnp.concatenate([p[i : i + 1] * column for p in parts], axis=0)
        total += jnp.dot(rows.astype(jnp.bfloat16), inc_ref[i], preferred_element_type=jnp.float32)
    return total[:SUB] + total[SUB : 2 * SUB] + total[2 * SUB :]


def put_load(load, load_ref, border_ref):
    slots = border_ref.shape[0]
    interior = load_ref.shape[0] - slots
    load_ref[...] = load[: load_ref.shape[0]]
    border_ref[...] = load[interior : interior + slots]


def start_kernel(pieces, *refs):
    ins, (onehot_ref, mask_ref, inc_ref, given_ref, flows_ref, load_ref, border_ref) = refs[:pieces], refs[pieces:]
    incs = inc_ref.shape[0]
    ins = [ins[-1], *ins[:-1]]
    rows = jnp.concatenate([ref[...] for ref in ins], axis=0)
    flows = pick_rows(onehot_ref[...], rows)
    flows_ref[...] = flows
    slots = given_ref.shape[0] // 2
    put_load(load_of(flows[:incs], mask_ref[...], inc_ref), load_ref, border_ref.at[:slots])
    border_ref[slots:] = given_ref[...]


def pick_kernel(pieces, blocks, incs, *refs):
    ins, (onehot_ref, limit_ref, utility_ref, same_ref) = refs[:pieces], refs[pieces:]
    group = 2 * blocks + SUB
    for offset, out in ((0, limit_ref), (blocks, utility_ref)):
        rows = [ref[k : k + blocks] for ref in ins for k in range(offset, ref.shape[0], group)]
        out[...] = pick_rows(onehot_ref[...], jnp.concatenate(rows, axis=0))
    owned = (lax.axis_index("shard") * blocks).astype(jnp.float32)
    own = lax.broadcasted_iota(jnp.int32, (blocks, 1), 0).astype(jnp.float32) + owned
    names = jnp.concatenate([column_of(ins[0][2 * blocks : 2 * blocks + 1, :incs]), own], axis=0)
    at = 0
    for ref in ins:
        for k in range(2 * blocks, ref.shape[0], group):
            same = jnp.where(names == ref[k : k + 1, :incs], 1.0, 0.0)
            same_ref[:, at : at + incs] = same.astype(jnp.bfloat16)
            at += incs


def flow_kernel(pieces, step_size, *refs):
    ins = refs[:pieces]
    ins = [ins[-1], ins[1], ins[0], *ins[2:-1]]
    (same_ref, flows_ref, limit_ref, utility_ref, mask_ref, inc_ref,
     out_ref, load_ref, border_ref) = refs[pieces:]
    terms = jnp.concatenate([ref[...] for ref in ins], axis=0)
    gradient = pick_rows(same_ref[...], terms)
    flows = flows_ref[...] - step_size * (gradient - utility_ref[...])
    flows = jnp.minimum(jnp.maximum(flows, 0.0), limit_ref[...])
    out_ref[...] = flows
    put_load(load_of(flows[: inc_ref.shape[0]], mask_ref[...], inc_ref), load_ref, border_ref)


def twin_of(ins, choice_ref):
    total = None
    for k, ref in enumerate(ins):
        term = jnp.where(choice_ref[k] > 0.5, ref[...], 0.0)
        total = term if total is None else total + term
    return total


def settle(ins, choice_ref, load_ref, limit, duals):
    load = load_ref[...]
    slots = ins[0].shape[0]
    interior = load.shape[0] - slots
    load = jnp.concatenate([load[:interior], load[interior:] + twin_of(ins, choice_ref)], axis=0)
    split = jnp.minimum(limit, load + duals)
    duals = (duals + load) - split
    return (load - split) + duals, duals


def back_terms(residual, mask, inc_ref, out_ref, turned=False):
    rows = residual.shape[0]
    if rows < SUB:
        residual = jnp.concatenate(
            [residual, jnp.zeros((SUB - rows, residual.shape[1]), jnp.float32)], axis=0
        )
    parts = [p.astype(jnp.float32) for p in split3(residual)]
    left = jnp.concatenate(parts, axis=0).astype(jnp.bfloat16)
    for i in range(inc_ref.shape[0]):
        dims = (((1,), (0 if turned else 1,)), ((), ()))
        got = lax.dot_general(left, inc_ref[i], dims, preferred_element_type=jnp.float32)
        got = got[:SUB] + got[SUB : 2 * SUB] + got[2 * SUB :]
        out_ref[i : i + 1, :] = jnp.sum(got * mask[:, i : i + 1], axis=0, keepdims=True)


def first_dual_kernel(others, unit, *refs):
    ins = refs[:others]
    (choice_ref, load_ref, cap_ref, dual_ref, mask_ref, inc_ref,
     limit_ref, out_ref, terms_ref) = refs[others:]
    slots = ins[0].shape[0] // 3
    interior = load_ref.shape[0] - slots
    loads, caps, starts = [[r.at[k * slots : (k + 1) * slots] for r in ins] for k in range(3)]

    def shared(ref, twins):
        mean = 0.5 * (ref[interior:] + twin_of(twins, choice_ref))
        return jnp.concatenate([ref[:interior], mean], axis=0)

    limit = unit * shared(cap_ref, caps)
    limit_ref[...] = limit
    residual, duals = settle(loads, choice_ref, load_ref, limit, shared(dual_ref, starts))
    out_ref[...] = duals
    back_terms(residual, mask_ref[...], inc_ref, terms_ref)


def dual_kernel(others, *refs):
    ins = refs[:others]
    (choice_ref, load_ref, limit_ref, dual_ref, mask_ref, inc_ref,
     out_ref, terms_ref) = refs[others:]
    residual, duals = settle(ins, choice_ref, load_ref, limit_ref[...], dual_ref[...])
    out_ref[...] = duals
    back_terms(residual, mask_ref[...], inc_ref, terms_ref, True)


def last_dual_kernel(others, *refs):
    ins = refs[:others]
    choice_ref, load_ref, limit_ref, dual_ref, out_ref = refs[others:]
    out_ref[...] = settle(ins, choice_ref, load_ref, limit_ref[...], dual_ref[...])[1]


def kernel_call(kernel, name, outs, operands, flops=0, scratch=(), space=pltpu.VMEM, grant=16):
    shapes = tuple(x if hasattr(x, "dtype") else jax.ShapeDtypeStruct(x, jnp.float32) for x in outs)
    size = sum(x.size * x.dtype.itemsize for x in operands)
    return pl.pallas_call(
        kernel,
        out_shape=shapes,
        in_specs=[pl.BlockSpec(memory_space=space)] * len(operands),
        out_specs=tuple(VMEM for _ in outs),
        scratch_shapes=scratch,
        compiler_params=pltpu.CompilerParams(vmem_limit_bytes=grant * 1024 * 1024),
        cost_estimate=pl.CostEstimate(flops=flops, bytes_accessed=size, transcendentals=0),
        name=name,
    )(*operands)


def body(
    flow_start,
    demand,
    utility,
    path_count,
    cluster_size,
    incidence,
    inc_path,
    inc_edge,
    capacity,
    dual_start,
    partner,
):
    blocks, width = flow_start.shape
    incs = incidence.shape[0]
    edges = incidence.shape[2]
    locals_ = capacity.shape[0]
    slots = partner.shape[1]
    clusters, devices = lax.axis_size("cluster"), lax.axis_size("shard")
    cluster, shard = lax.axis_index("cluster"), lax.axis_index("shard")
    rows = incs + blocks
    norm_bound = max(2, incs * incs * width * edges // (1024 * locals_ * blocks))
    unit = float(max(1, incs * width // (160 * locals_)))
    step_size = 1.0 / (2.0 * norm_bound)
    bits = devices.bit_length() - 1
    assert devices == 1 << bits and clusters & (clusters - 1) == 0
    stages = [1] * (bits % 2) + [2] * (bits // 2)

    def share(x, stages, shift=0, hold=None):
        pieces = x if isinstance(x, list) else [x]
        for step in stages:
            now = pieces[0] if len(pieces) == 1 else jnp.concatenate(pieces, axis=0)
            pieces = [now]
            for k in range(1, 1 << step):
                pairs = [(i, i ^ (k << shift)) for i in range(devices)]
                given = now if hold is None else tied(now, hold[min(len(hold), (1 << step) - k) - 1])
                pieces.append(lax.ppermute(given, "shard", pairs))
            shift += step
        return pieces

    def trade(x):
        return [
            lax.ppermute(x, "cluster", [(i, i ^ k) for i in range(clusters)])
            for k in range(1, clusters)
        ]

    half = jnp.bfloat16
    first, second, border, onehot, mask, choice = kernel_call(
        prep_kernel,
        "prepare",
        [
            (blocks, width),
            (2 * blocks + SUB, width),
            (2 * slots, edges),
            jax.ShapeDtypeStruct((rows, blocks * devices), half),
            (SUB, incs),
            (clusters - 1, slots, edges),
        ],
        [
            flow_start, demand, utility, capacity, dual_start, inc_path[None, :], inc_edge[None, :],
            path_count, cluster_size, partner,
        ],
        scratch=[
            pltpu.VMEM((blocks, width), jnp.float32),
            pltpu.VMEM((blocks, width), jnp.float32),
            pltpu.VMEM((locals_, edges), jnp.float32),
            pltpu.VMEM((locals_, edges), jnp.float32),
            pltpu.VMEM((1, incs), jnp.int32),
            pltpu.VMEM((1, incs), jnp.int32),
            pltpu.SMEM((blocks,), jnp.int32),
            pltpu.SMEM((1,), jnp.int32),
            pltpu.SMEM((1, slots), jnp.int32),
            pltpu.SemaphoreType.DMA((10,)),
        ],
        space=pltpu.HBM, grant=56,
    )

    def tied(x, *after):
        return lax.optimization_barrier((x, *after))[0]

    stages_first, stages_rest = stages[:1], stages[1:]
    firsts = share(first, stages_first)
    seconds = share(second, stages_first)
    inc = pl.pallas_call(
        cast_kernel,
        grid=(4,),
        in_specs=[pl.BlockSpec((incs // 4, width, edges), lambda k: (k, 0, 0))],
        out_specs=pl.BlockSpec((incs // 4, width, edges), lambda k: (k, 0, 0)),
        out_shape=jax.ShapeDtypeStruct(incidence.shape, half),
        compiler_params=pltpu.CompilerParams(vmem_limit_bytes=16 * 1024 * 1024),
        cost_estimate=pl.CostEstimate(flops=0, bytes_accessed=6 * incidence.size, transcendentals=0),
        name="cast",
    )(incidence)
    firsts = share(firsts, stages_rest, stages[0])

    others = clusters - 1
    flops = 2 * incs * width * edges * SUB
    load_shapes = [(rows, width), (locals_, edges), (slots, edges)]
    flows, load, out = kernel_call(
        lambda *refs: start_kernel(len(firsts), *refs), "first_load",
        [(rows, width), (locals_, edges), (3 * slots, edges)],
        [*firsts[1:], firsts[0], onehot, mask, inc, border], flops=flops,
    )
    dual_shape, term_shape = (locals_, edges), (incs, width)
    limit, duals, terms = kernel_call(
        lambda *refs: first_dual_kernel(others, unit, *refs), "first_duals",
        [dual_shape, dual_shape, term_shape],
        [*trade(out), choice, load, capacity, dual_start, mask, inc], flops=flops,
    )
    for iteration in range(ITERS):
        near = share(terms, stages_first)
        if iteration == 0:
            seconds = share(seconds, stages_rest, stages[0], [out, out, terms])
            (turned_inc,) = kernel_call(
                turn_kernel, "transpose", [jax.ShapeDtypeStruct((incs, edges, width), half)],
                [tied(inc, near[-1])],
            )
            limits, utilities, same = kernel_call(
                lambda *refs: pick_kernel(len(seconds), blocks, incs, *refs), "pick",
                [(rows, width)] * 2 + [jax.ShapeDtypeStruct((rows, incs * devices), half)],
                [*seconds, onehot],
            )
        far = share(near, stages_rest, stages[0])
        flows, load, out = kernel_call(
            lambda *refs: flow_kernel(len(firsts), step_size, *refs), "flows", load_shapes,
            [far[2], far[1], *far[3:], far[0], same, flows, limits, utilities, mask, inc], flops=flops,
        )
        operands = [*trade(out), choice, load, limit, duals]
        if iteration < ITERS - 1:
            duals, terms = kernel_call(
                lambda *refs: dual_kernel(others, *refs), "duals", [dual_shape, term_shape],
                [*operands, mask, turned_inc], flops=flops,
            )
    (duals,) = kernel_call(
        lambda *refs: last_dual_kernel(others, *refs), "last_duals", [dual_shape], operands
    )
    return flows[incs:], duals


def solution(mesh):
    whole = P(("cluster", "shard"))
    wide = P(("cluster", "shard"), None)
    return jax.shard_map(
        body,
        mesh=mesh,
        in_specs=(
            wide, wide, wide, whole, P("cluster"), P(("cluster", "shard"), None, None),
            whole, whole, wide, wide, P("cluster", None),
        ),
        out_specs=(wide, wide),
        check_vma=False,
    )
```

```python
import jax
import jax.numpy as jnp
from jax import lax
from jax.experimental import pallas as pl
from jax.experimental.pallas import tpu as pltpu
from jax.sharding import PartitionSpec as P

ITERS = 3
SUB = 8
VMEM = pl.BlockSpec(memory_space=pltpu.VMEM)


def split3(x):
    high = x.astype(jnp.bfloat16)
    rest = x - high.astype(jnp.float32)
    middle = rest.astype(jnp.bfloat16)
    low = (rest - middle.astype(jnp.float32)).astype(jnp.bfloat16)
    return high, middle, low


def pick_rows(onehot, rows):
    total = None
    for part in split3(rows):
        term = jnp.dot(onehot, part, preferred_element_type=jnp.float32)
        total = term if total is None else total + term
    return total


def column_of(row):
    n = row.shape[1]
    down = lax.broadcasted_iota(jnp.int32, (n, n), 0)
    along = lax.broadcasted_iota(jnp.int32, (n, n), 1)
    return jnp.sum(jnp.where(down == along, row, 0.0), axis=1, keepdims=True)


def prep_kernel(
    start_hbm, demand_hbm, utility_hbm, cap_hbm, dual_hbm, path_hbm, edge_hbm, count_hbm, size_hbm, partner_hbm,
    first_ref, second_ref, border_ref, onehot_ref, mask_ref, choice_ref,
    start_ref, demand_ref, cap_ref, dual_ref, path_ref, edge_ref, count_ref, size_ref, partner_ref, sems,
):
    blocks, width = start_ref.shape
    slots = border_ref.shape[0] // 2
    interior = cap_ref.shape[0] - slots
    incs = path_ref.shape[1]
    copies = [
        pltpu.make_async_copy(source, target, sems.at[k])
        for k, (source, target) in enumerate(
            [
                (start_hbm, start_ref),
                (demand_hbm, demand_ref),
                (utility_hbm, second_ref.at[blocks : 2 * blocks]),
                (cap_hbm, cap_ref),
                (dual_hbm, dual_ref),
                (path_hbm, path_ref),
                (edge_hbm, edge_ref),
                (count_hbm, count_ref),
                (size_hbm, size_ref),
                (partner_hbm, partner_ref),
            ]
        )
    ]
    for copy in copies:
        copy.start()
    cluster, shard = lax.axis_index("cluster"), lax.axis_index("shard")
    for copy in copies:
        copy.wait()
    lanes = lax.broadcasted_iota(jnp.int32, (1, width), 1)
    limits = []
    for j in range(blocks):
        count = jnp.where(j < size_ref[0], count_ref[j], 0)
        limits.append(jnp.where(lanes < count, demand_ref[j : j + 1, :], 0.0))
    limit = jnp.concatenate(limits, axis=0)
    first_ref[:blocks] = jnp.minimum(jnp.maximum(start_ref[...], 0.0), limit)
    second_ref[:blocks] = limit
    names = path_ref[...]
    first_ref[blocks:] = jnp.zeros((SUB, width), jnp.float32)
    first_ref[blocks : blocks + 1, :incs] = names.astype(jnp.float32)
    border_ref[:slots] = cap_ref[interior:]
    border_ref[slots:] = dual_ref[interior:]
    place = jnp.bitwise_xor(names // blocks, shard) * blocks + names % blocks
    total = onehot_ref.shape[1]
    along = lax.broadcasted_iota(jnp.int32, (incs, total), 1).astype(jnp.float32)
    picked = jnp.where(along == column_of(place.astype(jnp.float32)), 1.0, 0.0)
    down = lax.broadcasted_iota(jnp.int32, (blocks, total), 0)
    own = jnp.where(down == lax.broadcasted_iota(jnp.int32, (blocks, total), 1), 1.0, 0.0)
    onehot_ref[...] = jnp.concatenate([picked, own], axis=0).astype(jnp.bfloat16)
    edge = lax.broadcasted_iota(jnp.int32, mask_ref.shape, 0)
    mask_ref[...] = jnp.where(edge == edge_ref[...], 1.0, 0.0)
    for k in range(choice_ref.shape[0]):
        for j in range(slots):
            chosen = jnp.where(partner_ref[0, j] == jnp.bitwise_xor(cluster, k + 1), 1.0, 0.0)
            choice_ref[k, j : j + 1, :] = jnp.full((1, choice_ref.shape[2]), chosen, jnp.float32)


def cast_kernel(inc_ref, out_ref):
    out_ref[...] = inc_ref[...].astype(jnp.bfloat16)


def turn_kernel(inc_ref, out_ref):
    for i in range(inc_ref.shape[0]):
        out_ref[i] = inc_ref[i].T


def load_of(flows, mask, inc_ref):
    count, _, edges = inc_ref.shape
    parts = [p.astype(jnp.float32) for p in split3(flows)]
    total = jnp.zeros((3 * SUB, edges), jnp.float32)
    for i in range(count):
        column = mask[:, i : i + 1]
        rows = jnp.concatenate([p[i : i + 1] * column for p in parts], axis=0)
        total += jnp.dot(rows.astype(jnp.bfloat16), inc_ref[i], preferred_element_type=jnp.float32)
    return total[:SUB] + total[SUB : 2 * SUB] + total[2 * SUB :]


def put_load(load, load_ref, border_ref):
    slots = border_ref.shape[0]
    interior = load_ref.shape[0] - slots
    load_ref[...] = load[: load_ref.shape[0]]
    border_ref[...] = load[interior : interior + slots]


def start_kernel(pieces, *refs):
    ins, (onehot_ref, mask_ref, inc_ref, given_ref, flows_ref, load_ref, border_ref) = refs[:pieces], refs[pieces:]
    incs = inc_ref.shape[0]
    ins = [ins[-1], *ins[:-1]]
    blocks = flows_ref.shape[0] - incs
    group = blocks + SUB
    rows = [ref[k : k + blocks] for ref in ins for k in range(0, ref.shape[0], group)]
    flows = pick_rows(onehot_ref[...], jnp.concatenate(rows, axis=0))
    flows_ref[...] = flows
    slots = given_ref.shape[0] // 2
    put_load(load_of(flows[:incs], mask_ref[...], inc_ref), load_ref, border_ref.at[:slots])
    border_ref[slots:] = given_ref[...]


def pick_kernel(pieces, blocks, *refs):
    ins, (onehot_ref, limit_ref, utility_ref) = refs[:pieces], refs[pieces:]
    for offset, out in ((0, limit_ref), (blocks, utility_ref)):
        rows = [ref[k : k + blocks] for ref in ins for k in range(offset, ref.shape[0], 2 * blocks)]
        out[...] = pick_rows(onehot_ref[...], jnp.concatenate(rows, axis=0))


def relate_kernel(pieces, blocks, incs, stride, *refs):
    ins, same_ref = refs[:pieces], refs[pieces]
    rows = incs + blocks
    group = blocks + SUB
    shard = lax.axis_index("shard")
    names = [ins[0][k : k + 1, :incs] for k in range(blocks, ins[0].shape[0], group)]
    names = jnp.concatenate(names, axis=1)
    down = lax.broadcasted_iota(jnp.int32, (blocks, 1), 0)
    for k, ref in enumerate(ins):
        own = (down + jnp.bitwise_xor(shard, k * stride) * blocks).astype(jnp.float32)
        wanted = jnp.concatenate([column_of(ref[blocks : blocks + 1, :incs]), own], axis=0)
        same_ref[k * rows : (k + 1) * rows] = jnp.where(wanted == names, 1.0, 0.0).astype(jnp.bfloat16)


def sum_kernel(pieces, *refs):
    ins, same_ref, outs = refs[:pieces], refs[pieces], refs[pieces + 1 :]
    terms = jnp.concatenate([ref[...] for ref in ins], axis=0)
    total = pick_rows(same_ref[...], terms)
    rows = outs[0].shape[0]
    for k, out in enumerate(outs):
        out[...] = total[k * rows : (k + 1) * rows]


def flow_kernel(pieces, step_size, *refs):
    ins = refs[:pieces]
    (flows_ref, limit_ref, utility_ref, mask_ref, inc_ref,
     out_ref, load_ref, border_ref) = refs[pieces:]
    gradient = ins[0][...]
    for ref in ins[1:]:
        gradient += ref[...]
    flows = flows_ref[...] - step_size * (gradient - utility_ref[...])
    flows = jnp.minimum(jnp.maximum(flows, 0.0), limit_ref[...])
    out_ref[...] = flows
    put_load(load_of(flows[: inc_ref.shape[0]], mask_ref[...], inc_ref), load_ref, border_ref)


def twin_of(ins, choice_ref):
    total = None
    for k, ref in enumerate(ins):
        term = jnp.where(choice_ref[k] > 0.5, ref[...], 0.0)
        total = term if total is None else total + term
    return total


def settle(ins, choice_ref, load_ref, limit, duals):
    load = load_ref[...]
    slots = ins[0].shape[0]
    interior = load.shape[0] - slots
    load = jnp.concatenate([load[:interior], load[interior:] + twin_of(ins, choice_ref)], axis=0)
    split = jnp.minimum(limit, load + duals)
    duals = (duals + load) - split
    return (load - split) + duals, duals


def back_terms(residual, mask, inc_ref, out_ref, turned=False):
    rows = residual.shape[0]
    if rows < SUB:
        residual = jnp.concatenate(
            [residual, jnp.zeros((SUB - rows, residual.shape[1]), jnp.float32)], axis=0
        )
    parts = [p.astype(jnp.float32) for p in split3(residual)]
    left = jnp.concatenate(parts, axis=0).astype(jnp.bfloat16)
    for i in range(inc_ref.shape[0]):
        dims = (((1,), (0 if turned else 1,)), ((), ()))
        got = lax.dot_general(left, inc_ref[i], dims, preferred_element_type=jnp.float32)
        got = got[:SUB] + got[SUB : 2 * SUB] + got[2 * SUB :]
        out_ref[i : i + 1, :] = jnp.sum(got * mask[:, i : i + 1], axis=0, keepdims=True)


def first_dual_kernel(others, unit, *refs):
    ins = refs[:others]
    (choice_ref, load_ref, cap_ref, dual_ref, mask_ref, inc_ref,
     limit_ref, out_ref, terms_ref) = refs[others:]
    slots = ins[0].shape[0] // 3
    interior = load_ref.shape[0] - slots
    loads, caps, starts = [[r.at[k * slots : (k + 1) * slots] for r in ins] for k in range(3)]

    def shared(ref, twins):
        mean = 0.5 * (ref[interior:] + twin_of(twins, choice_ref))
        return jnp.concatenate([ref[:interior], mean], axis=0)

    limit = unit * shared(cap_ref, caps)
    limit_ref[...] = limit
    residual, duals = settle(loads, choice_ref, load_ref, limit, shared(dual_ref, starts))
    out_ref[...] = duals
    back_terms(residual, mask_ref[...], inc_ref, terms_ref)


def dual_kernel(others, *refs):
    ins = refs[:others]
    (choice_ref, load_ref, limit_ref, dual_ref, mask_ref, inc_ref,
     out_ref, terms_ref) = refs[others:]
    residual, duals = settle(ins, choice_ref, load_ref, limit_ref[...], dual_ref[...])
    out_ref[...] = duals
    back_terms(residual, mask_ref[...], inc_ref, terms_ref, True)


def last_dual_kernel(others, *refs):
    ins = refs[:others]
    choice_ref, load_ref, limit_ref, dual_ref, out_ref = refs[others:]
    out_ref[...] = settle(ins, choice_ref, load_ref, limit_ref[...], dual_ref[...])[1]


def kernel_call(kernel, name, outs, operands, flops=0, scratch=(), space=pltpu.VMEM, grant=16):
    shapes = tuple(x if hasattr(x, "dtype") else jax.ShapeDtypeStruct(x, jnp.float32) for x in outs)
    size = sum(x.size * x.dtype.itemsize for x in operands)
    return pl.pallas_call(
        kernel,
        out_shape=shapes,
        in_specs=[pl.BlockSpec(memory_space=space)] * len(operands),
        out_specs=tuple(VMEM for _ in outs),
        scratch_shapes=scratch,
        compiler_params=pltpu.CompilerParams(vmem_limit_bytes=grant * 1024 * 1024),
        cost_estimate=pl.CostEstimate(flops=flops, bytes_accessed=size, transcendentals=0),
        name=name,
    )(*operands)


def body(
    flow_start,
    demand,
    utility,
    path_count,
    cluster_size,
    incidence,
    inc_path,
    inc_edge,
    capacity,
    dual_start,
    partner,
):
    blocks, width = flow_start.shape
    incs = incidence.shape[0]
    edges = incidence.shape[2]
    locals_ = capacity.shape[0]
    slots = partner.shape[1]
    clusters, devices = lax.axis_size("cluster"), lax.axis_size("shard")
    cluster, shard = lax.axis_index("cluster"), lax.axis_index("shard")
    rows = incs + blocks
    norm_bound = max(2, incs * incs * width * edges // (1024 * locals_ * blocks))
    unit = float(max(1, incs * width // (160 * locals_)))
    step_size = 1.0 / (2.0 * norm_bound)
    bits = devices.bit_length() - 1
    assert devices == 1 << bits and clusters & (clusters - 1) == 0
    stages = [1] * (bits % 2) + [2] * (bits // 2)

    def share(x, stages, shift=0, hold=None):
        pieces = x if isinstance(x, list) else [x]
        for step in stages:
            now = pieces[0] if len(pieces) == 1 else jnp.concatenate(pieces, axis=0)
            pieces = [now]
            for k in range(1, 1 << step):
                pairs = [(i, i ^ (k << shift)) for i in range(devices)]
                given = now if hold is None else tied(now, hold[min(len(hold), (1 << step) - k) - 1])
                pieces.append(lax.ppermute(given, "shard", pairs))
            shift += step
        return pieces

    def trade(x):
        return [
            lax.ppermute(x, "cluster", [(i, i ^ k) for i in range(clusters)])
            for k in range(1, clusters)
        ]

    half = jnp.bfloat16
    first, second, border, onehot, mask, choice = kernel_call(
        prep_kernel,
        "prepare",
        [
            (blocks + SUB, width),
            (2 * blocks, width),
            (2 * slots, edges),
            jax.ShapeDtypeStruct((rows, blocks * devices), half),
            (SUB, incs),
            (clusters - 1, slots, edges),
        ],
        [
            flow_start, demand, utility, capacity, dual_start, inc_path[None, :], inc_edge[None, :],
            path_count, cluster_size, partner,
        ],
        scratch=[
            pltpu.VMEM((blocks, width), jnp.float32),
            pltpu.VMEM((blocks, width), jnp.float32),
            pltpu.VMEM((locals_, edges), jnp.float32),
            pltpu.VMEM((locals_, edges), jnp.float32),
            pltpu.VMEM((1, incs), jnp.int32),
            pltpu.VMEM((1, incs), jnp.int32),
            pltpu.SMEM((blocks,), jnp.int32),
            pltpu.SMEM((1,), jnp.int32),
            pltpu.SMEM((1, slots), jnp.int32),
            pltpu.SemaphoreType.DMA((10,)),
        ],
        space=pltpu.HBM, grant=56,
    )

    def tied(x, *after):
        return lax.optimization_barrier((x, *after))[0]

    stages_first, stages_rest = stages[:1], stages[1:]
    firsts = share(first, stages_first)
    seconds = share(second, stages_first)
    inc = pl.pallas_call(
        cast_kernel,
        grid=(4,),
        in_specs=[pl.BlockSpec((incs // 4, width, edges), lambda k: (k, 0, 0))],
        out_specs=pl.BlockSpec((incs // 4, width, edges), lambda k: (k, 0, 0)),
        out_shape=jax.ShapeDtypeStruct(incidence.shape, half),
        compiler_params=pltpu.CompilerParams(vmem_limit_bytes=16 * 1024 * 1024),
        cost_estimate=pl.CostEstimate(flops=0, bytes_accessed=6 * incidence.size, transcendentals=0),
        name="cast",
    )(tied(incidence, firsts[-1]))
    firsts = share(firsts, stages_rest, stages[0])
    far_count, stride = 1 << stages[-1], devices >> stages[-1]
    (same,) = kernel_call(
        lambda *refs: relate_kernel(far_count, blocks, incs, stride, *refs), "relate",
        [jax.ShapeDtypeStruct((far_count * rows, incs * stride), half)], firsts,
    )

    others = clusters - 1
    flops = 2 * incs * width * edges * SUB
    load_shapes = [(rows, width), (locals_, edges), (slots, edges)]
    flows, load, out = kernel_call(
        lambda *refs: start_kernel(len(firsts), *refs), "first_load",
        [(rows, width), (locals_, edges), (3 * slots, edges)],
        [*firsts[1:], firsts[0], onehot, mask, inc, border], flops=flops,
    )
    dual_shape, term_shape = (locals_, edges), (incs, width)
    limit, duals, terms = kernel_call(
        lambda *refs: first_dual_kernel(others, unit, *refs), "first_duals",
        [dual_shape, dual_shape, term_shape],
        [*trade(out), choice, load, capacity, dual_start, mask, inc], flops=flops,
    )
    for iteration in range(ITERS):
        near = share(terms, stages[:-1])
        if iteration == 0:
            seconds = share(seconds, stages_rest, stages[0], [out, out, terms])
            (turned_inc,) = kernel_call(
                turn_kernel, "transpose", [jax.ShapeDtypeStruct((incs, edges, width), half)],
                [tied(inc, near[-1])],
            )
            limits, utilities = kernel_call(
                lambda *refs: pick_kernel(len(seconds), blocks, *refs), "pick", [(rows, width)] * 2,
                [*seconds, onehot],
            )
        sums = kernel_call(
            lambda *refs: sum_kernel(len(near), *refs), "sums", [(rows, width)] * far_count,
            [*near, same],
        )
        far = [sums[0]] + [
            lax.ppermute(x, "shard", [(i, i ^ (k * stride)) for i in range(devices)])
            for k, x in enumerate(sums) if k > 0
        ]
        flows, load, out = kernel_call(
            lambda *refs: flow_kernel(len(far), step_size, *refs), "flows", load_shapes,
            [far[2], far[3], far[1], far[0], flows, limits, utilities, mask, inc], flops=flops,
        )
        operands = [*trade(out), choice, load, limit, duals]
        if iteration < ITERS - 1:
            duals, terms = kernel_call(
                lambda *refs: dual_kernel(others, *refs), "duals", [dual_shape, term_shape],
                [*operands, mask, turned_inc], flops=flops,
            )
    (duals,) = kernel_call(
        lambda *refs: last_dual_kernel(others, *refs), "last_duals", [dual_shape], operands
    )
    return flows[incs:], duals


def solution(mesh):
    whole = P(("cluster", "shard"))
    wide = P(("cluster", "shard"), None)
    return jax.shard_map(
        body,
        mesh=mesh,
        in_specs=(
            wide, wide, wide, whole, P("cluster"), P(("cluster", "shard"), None, None),
            whole, whole, wide, wide, P("cluster", None),
        ),
        out_specs=(wide, wide),
        check_vma=False,
    )
```

```python
import jax
import jax.numpy as jnp
from jax import lax
from jax.experimental import pallas as pl
from jax.experimental.pallas import tpu as pltpu
from jax.sharding import PartitionSpec as P

ITERS = 3
SUB = 8
VMEM = pl.BlockSpec(memory_space=pltpu.VMEM)


def split3(x):
    high = x.astype(jnp.bfloat16)
    rest = x - high.astype(jnp.float32)
    middle = rest.astype(jnp.bfloat16)
    low = (rest - middle.astype(jnp.float32)).astype(jnp.bfloat16)
    return high, middle, low


def pick_rows(onehot, rows):
    total = None
    for part in split3(rows):
        term = jnp.dot(onehot, part, preferred_element_type=jnp.float32)
        total = term if total is None else total + term
    return total


def column_of(row):
    n = row.shape[1]
    down = lax.broadcasted_iota(jnp.int32, (n, n), 0)
    along = lax.broadcasted_iota(jnp.int32, (n, n), 1)
    return jnp.sum(jnp.where(down == along, row, 0.0), axis=1, keepdims=True)


def pick_thrice(thrice, rows):
    parts = jnp.concatenate(split3(rows), axis=0)
    return jnp.dot(thrice, parts, preferred_element_type=jnp.float32)


def copy_all(pairs, sems):
    copies = [pltpu.make_async_copy(*pair, sems.at[k]) for k, pair in enumerate(pairs)]
    for copy in copies:
        copy.start()
    for copy in copies:
        copy.wait()


def prep_kernel(
    start_hbm, demand_hbm, utility_hbm, path_hbm, count_hbm, size_hbm,
    first_ref, start_ref, demand_ref, path_ref, count_ref, size_ref, sems,
):
    blocks, width = start_ref.shape
    incs = path_ref.shape[1]
    copy_all(
        [
            (start_hbm, start_ref),
            (demand_hbm, demand_ref),
            (utility_hbm, first_ref.at[2 * blocks + SUB :]),
            (path_hbm, path_ref),
            (count_hbm, count_ref),
            (size_hbm, size_ref),
        ],
        sems,
    )
    lanes = lax.broadcasted_iota(jnp.int32, (1, width), 1)
    limits = []
    for j in range(blocks):
        count = jnp.where(j < size_ref[0], count_ref[j], 0)
        limits.append(jnp.where(lanes < count, demand_ref[j : j + 1, :], 0.0))
    limit = jnp.concatenate(limits, axis=0)
    first_ref[:blocks] = jnp.minimum(jnp.maximum(start_ref[...], 0.0), limit)
    first_ref[blocks : 2 * blocks] = limit
    first_ref[2 * blocks : 2 * blocks + SUB] = jnp.zeros((SUB, width), jnp.float32)
    first_ref[2 * blocks : 2 * blocks + 1, :incs] = path_ref[...].astype(jnp.float32)


def table_kernel(
    path_hbm, edge_hbm, partner_hbm,
    onehot_ref, mask_ref, choice_ref, path_ref, edge_ref, partner_ref, sems,
):
    incs = path_ref.shape[1]
    blocks = onehot_ref.shape[0] - incs
    cluster, shard = lax.axis_index("cluster"), lax.axis_index("shard")
    copy_all([(path_hbm, path_ref), (edge_hbm, edge_ref), (partner_hbm, partner_ref)], sems)
    names = path_ref[...]
    place = jnp.bitwise_xor(names // blocks, shard) * blocks + names % blocks
    total = onehot_ref.shape[1]
    along = lax.broadcasted_iota(jnp.int32, (incs, total), 1).astype(jnp.float32)
    picked = jnp.where(along == column_of(place.astype(jnp.float32)), 1.0, 0.0)
    down = lax.broadcasted_iota(jnp.int32, (blocks, total), 0)
    own = jnp.where(down == lax.broadcasted_iota(jnp.int32, (blocks, total), 1), 1.0, 0.0)
    onehot_ref[...] = jnp.concatenate([picked, own], axis=0).astype(jnp.bfloat16)
    edge = lax.broadcasted_iota(jnp.int32, mask_ref.shape, 0)
    mask_ref[...] = jnp.where(edge == edge_ref[...], 1.0, 0.0)
    for k in range(choice_ref.shape[0]):
        for j in range(partner_ref.shape[1]):
            chosen = jnp.where(partner_ref[0, j] == jnp.bitwise_xor(cluster, k + 1), 1.0, 0.0)
            choice_ref[k, j : j + 1, :] = jnp.full((1, choice_ref.shape[2]), chosen, jnp.float32)


def cast_kernel(inc_ref, out_ref):
    out_ref[...] = inc_ref[...].astype(jnp.bfloat16)


def turn_kernel(inc_ref, out_ref):
    for i in range(inc_ref.shape[0]):
        out_ref[i] = inc_ref[i].T


def load_of(flows, mask, inc_ref):
    count, _, edges = inc_ref.shape
    parts = [p.astype(jnp.float32) for p in split3(flows)]
    total = jnp.zeros((3 * SUB, edges), jnp.float32)
    for i in range(count):
        column = mask[:, i : i + 1]
        rows = jnp.concatenate([p[i : i + 1] * column for p in parts], axis=0)
        total += jnp.dot(rows.astype(jnp.bfloat16), inc_ref[i], preferred_element_type=jnp.float32)
    return total[:SUB] + total[SUB : 2 * SUB] + total[2 * SUB :]


def put_load(load, load_ref, border_ref):
    slots = border_ref.shape[0]
    interior = load_ref.shape[0] - slots
    load_ref[...] = load[: load_ref.shape[0]]
    border_ref[...] = load[interior : interior + slots]


def offsets(ref, blocks):
    return [0, *range(2 * blocks + SUB, ref.shape[0], 2 * blocks)]


def start_kernel(pieces, *refs):
    ins, (onehot_ref, mask_ref, inc_ref, cap_ref, dual_ref, flows_ref, load_ref, border_ref) = refs[:pieces], refs[pieces:]
    incs = inc_ref.shape[0]
    ins = [ins[-1], *ins[:-1]]
    blocks = flows_ref.shape[0] - incs
    rows = [ref[k : k + blocks] for ref in ins for k in offsets(ref, blocks)]
    flows = pick_rows(onehot_ref[...], jnp.concatenate(rows, axis=0))
    flows_ref[...] = flows
    slots = border_ref.shape[0] // 3
    interior = cap_ref.shape[0] - slots
    put_load(load_of(flows[:incs], mask_ref[...], inc_ref), load_ref, border_ref.at[:slots])
    border_ref[slots : 2 * slots] = cap_ref[interior:]
    border_ref[2 * slots :] = dual_ref[interior:]


def pick_kernel(pieces, blocks, *refs):
    ins, (onehot_ref, limit_ref) = refs[:pieces], refs[pieces:]
    rows = [ref[k + blocks : k + 2 * blocks] for ref in ins for k in offsets(ref, blocks)]
    limit_ref[...] = pick_rows(onehot_ref[...], jnp.concatenate(rows, axis=0))


def relate_kernel(pieces, blocks, incs, stride, *refs):
    ins, near, (own_ref, others_ref) = refs[:pieces], refs[pieces:-2], refs[-2:]
    rows = incs + blocks
    shard = lax.axis_index("shard")
    at = 2 * blocks
    group = 3 * blocks + SUB
    names = [ref[k : k + 1, :incs] for ref in near for k in range(at, ref.shape[0], group)]
    along = lax.broadcasted_iota(jnp.int32, (1, blocks), 1)
    owned = [
        (along + jnp.bitwise_xor(shard, k) * blocks).astype(jnp.float32) for k in range(stride)
    ]
    others = jnp.concatenate(names[1:] * 3, axis=1)
    here = jnp.concatenate([names[0], *owned] * 3, axis=1)
    column = lax.broadcasted_iota(jnp.int32, here.shape, 1) % (incs + stride * blocks)
    weight = jnp.where(column < incs, 1.0, -1.0)
    down = lax.broadcasted_iota(jnp.int32, (blocks, 1), 0)
    for k, ref in enumerate(ins):
        own = (down + jnp.bitwise_xor(shard, k * stride) * blocks).astype(jnp.float32)
        wanted = column_of(ref[2 * blocks : 2 * blocks + 1, :incs])
        wanted = jnp.concatenate([wanted, own], axis=0)
        place = slice(k * rows, (k + 1) * rows)
        own_ref[place] = jnp.where(wanted == here, weight, 0.0).astype(jnp.bfloat16)
        others_ref[place] = jnp.where(wanted == others, 1.0, 0.0).astype(jnp.bfloat16)


def part_kernel(terms_ref, *refs):
    ins, (own_ref, out_ref) = refs[:-2], refs[-2:]
    rows = jnp.concatenate([terms_ref[...], *[ref[...] for ref in ins]], axis=0)
    out_ref[...] = pick_thrice(own_ref[...], rows)


def sum_kernel(pieces, skip, *refs):
    ins, (others_ref, part_ref), outs = refs[:pieces], refs[pieces : pieces + 2], refs[pieces + 2 :]
    terms = jnp.concatenate([ref[...] for ref in ins], axis=0)[skip:]
    total = part_ref[...] + pick_thrice(others_ref[...], terms)
    rows = outs[0].shape[0]
    for k, out in enumerate(outs):
        out[...] = total[k * rows : (k + 1) * rows]


def flow_kernel(pieces, step_size, *refs):
    ins = refs[:pieces]
    flows_ref, limit_ref, mask_ref, inc_ref, out_ref, load_ref, border_ref = refs[pieces:]
    slope = ins[0][...]
    for ref in ins[1:]:
        slope += ref[...]
    flows = flows_ref[...] - step_size * slope
    flows = jnp.minimum(jnp.maximum(flows, 0.0), limit_ref[...])
    out_ref[...] = flows
    put_load(load_of(flows[: inc_ref.shape[0]], mask_ref[...], inc_ref), load_ref, border_ref)


def twin_of(ins, choice_ref):
    total = None
    for k, ref in enumerate(ins):
        term = jnp.where(choice_ref[k] > 0.5, ref[...], 0.0)
        total = term if total is None else total + term
    return total


def settle(ins, choice_ref, load_ref, limit, duals):
    load = load_ref[...]
    slots = ins[0].shape[0]
    interior = load.shape[0] - slots
    load = jnp.concatenate([load[:interior], load[interior:] + twin_of(ins, choice_ref)], axis=0)
    split = jnp.minimum(limit, load + duals)
    duals = (duals + load) - split
    return (load - split) + duals, duals


def back_terms(residual, mask, inc_ref, out_ref):
    rows = residual.shape[0]
    if rows < SUB:
        residual = jnp.concatenate(
            [residual, jnp.zeros((SUB - rows, residual.shape[1]), jnp.float32)], axis=0
        )
    parts = [p.astype(jnp.float32) for p in split3(residual)]
    left = jnp.concatenate(parts, axis=0).astype(jnp.bfloat16)
    for i in range(inc_ref.shape[0]):
        got = jnp.dot(left, inc_ref[i], preferred_element_type=jnp.float32)
        got = got[:SUB] + got[SUB : 2 * SUB] + got[2 * SUB :]
        out_ref[i : i + 1, :] = jnp.sum(got * mask[:, i : i + 1], axis=0, keepdims=True)


def first_dual_kernel(others, unit, *refs):
    ins = refs[:others]
    (choice_ref, load_ref, cap_ref, dual_ref, mask_ref, inc_ref,
     limit_ref, out_ref, terms_ref) = refs[others:]
    slots = ins[0].shape[0] // 3
    interior = load_ref.shape[0] - slots
    loads, caps, starts = [[r.at[k * slots : (k + 1) * slots] for r in ins] for k in range(3)]

    def shared(ref, twins):
        mean = 0.5 * (ref[interior:] + twin_of(twins, choice_ref))
        return jnp.concatenate([ref[:interior], mean], axis=0)

    limit = unit * shared(cap_ref, caps)
    limit_ref[...] = limit
    residual, duals = settle(loads, choice_ref, load_ref, limit, shared(dual_ref, starts))
    out_ref[...] = duals
    back_terms(residual, mask_ref[...], inc_ref, terms_ref)


def dual_kernel(others, *refs):
    ins = refs[:others]
    (choice_ref, load_ref, limit_ref, dual_ref, mask_ref, inc_ref,
     out_ref, terms_ref) = refs[others:]
    residual, duals = settle(ins, choice_ref, load_ref, limit_ref[...], dual_ref[...])
    out_ref[...] = duals
    back_terms(residual, mask_ref[...], inc_ref, terms_ref)


def last_dual_kernel(others, *refs):
    ins = refs[:others]
    choice_ref, load_ref, limit_ref, dual_ref, out_ref = refs[others:]
    out_ref[...] = settle(ins, choice_ref, load_ref, limit_ref[...], dual_ref[...])[1]


def kernel_call(kernel, name, outs, operands, flops=0, scratch=(), pin=False):
    shapes = tuple(x if hasattr(x, "dtype") else jax.ShapeDtypeStruct(x, jnp.float32) for x in outs)
    size = sum(x.size * x.dtype.itemsize for x in operands)
    if pin:
        operands = [pltpu.with_memory_space_constraint(x, pltpu.HBM) if x.size > 1 else x for x in operands]
    return pl.pallas_call(
        kernel,
        out_shape=shapes,
        in_specs=[pl.BlockSpec(memory_space=pltpu.HBM if pin else pltpu.VMEM)] * len(operands),
        out_specs=tuple(VMEM for _ in outs),
        scratch_shapes=scratch,
        compiler_params=pltpu.CompilerParams(vmem_limit_bytes=16 * 1024 * 1024),
        cost_estimate=pl.CostEstimate(flops=flops, bytes_accessed=size, transcendentals=0),
        name=name,
    )(*operands)


def body(
    flow_start,
    demand,
    utility,
    path_count,
    cluster_size,
    incidence,
    inc_path,
    inc_edge,
    capacity,
    dual_start,
    partner,
):
    blocks, width = flow_start.shape
    incs = incidence.shape[0]
    edges = incidence.shape[2]
    locals_ = capacity.shape[0]
    slots = partner.shape[1]
    clusters, devices = lax.axis_size("cluster"), lax.axis_size("shard")
    cluster, shard = lax.axis_index("cluster"), lax.axis_index("shard")
    rows = incs + blocks
    norm_bound = max(2, incs * incs * width * edges // (1024 * locals_ * blocks))
    unit = float(max(1, incs * width // (160 * locals_)))
    step_size = 1.0 / (2.0 * norm_bound)
    bits = devices.bit_length() - 1
    assert devices == 1 << bits and clusters & (clusters - 1) == 0
    stages = [1] * (bits % 2) + [2] * (bits // 2)

    def share(x, stages, shift=0, hold=None):
        pieces = x if isinstance(x, list) else [x]
        for step in stages:
            now = pieces[0] if len(pieces) == 1 else jnp.concatenate(pieces, axis=0)
            pieces = [now]
            for k in range(1, 1 << step):
                pairs = [(i, i ^ (k << shift)) for i in range(devices)]
                given = now if hold is None else tied(now, hold[min(len(hold), (1 << step) - k) - 1])
                pieces.append(lax.ppermute(given, "shard", pairs))
            shift += step
        return pieces

    def trade(x):
        return [
            lax.ppermute(x, "cluster", [(i, i ^ k) for i in range(clusters)])
            for k in range(1, clusters)
        ]

    def tied(x, *after):
        return lax.optimization_barrier((x, *after))[0]

    stages_first, stages_rest = stages[:1], stages[1:]
    half = jnp.bfloat16
    (first,) = kernel_call(
        prep_kernel,
        "prepare",
        [(3 * blocks + SUB, width)],
        [flow_start, demand, utility, inc_path[None, :], path_count, cluster_size],
        scratch=[
            pltpu.VMEM((blocks, width), jnp.float32),
            pltpu.VMEM((blocks, width), jnp.float32),
            pltpu.VMEM((1, incs), jnp.int32),
            pltpu.SMEM((blocks,), jnp.int32),
            pltpu.SMEM((1,), jnp.int32),
            pltpu.SemaphoreType.DMA((6,)),
        ],
        pin=True,
    )
    onehot, mask, choice = kernel_call(
        table_kernel,
        "tables",
        [
            jax.ShapeDtypeStruct((rows, blocks * devices), half),
            (SUB, incs),
            (clusters - 1, slots, edges),
        ],
        [tied(inc_path, first)[None, :], inc_edge[None, :], partner],
        scratch=[
            pltpu.VMEM((1, incs), jnp.int32),
            pltpu.VMEM((1, incs), jnp.int32),
            pltpu.SMEM((1, slots), jnp.int32),
            pltpu.SemaphoreType.DMA((3,)),
        ],
        pin=True,
    )

    limits_end, kept = 2 * blocks, 2 * blocks + SUB
    near_firsts = share(first, stages[:-1])
    groups = [p[k : k + kept + blocks] for p in near_firsts for k in range(0, p.shape[0], kept + blocks)]
    utilities = [p[kept:] for p in groups]
    firsts = [jnp.concatenate([groups[0][:kept], *[p[:limits_end] for p in groups[1:]]], axis=0)]
    inc = pl.pallas_call(
        cast_kernel,
        grid=(4,),
        in_specs=[pl.BlockSpec((incs // 4, width, edges), lambda k: (k, 0, 0))],
        out_specs=pl.BlockSpec((incs // 4, width, edges), lambda k: (k, 0, 0)),
        out_shape=jax.ShapeDtypeStruct(incidence.shape, half),
        compiler_params=pltpu.CompilerParams(vmem_limit_bytes=16 * 1024 * 1024),
        cost_estimate=pl.CostEstimate(flops=0, bytes_accessed=6 * incidence.size, transcendentals=0),
        name="cast",
    )(tied(incidence, firsts[-1]))
    firsts = share(firsts, stages[-1:], bits - stages[-1])
    far_count, stride = 1 << stages[-1], devices >> stages[-1]
    own_same, other_same = kernel_call(
        lambda *refs: relate_kernel(far_count, blocks, incs, stride, *refs), "relate",
        [
            jax.ShapeDtypeStruct((far_count * rows, 3 * (incs + stride * blocks)), half),
            jax.ShapeDtypeStruct((far_count * rows, 3 * incs * (stride - 1)), half),
        ],
        [*firsts, *near_firsts],
    )

    others = clusters - 1
    flops = 2 * incs * width * edges * SUB
    load_shapes = [(rows, width), (locals_, edges), (slots, edges)]
    flows, load, out = kernel_call(
        lambda *refs: start_kernel(len(firsts), *refs), "first_load",
        [(rows, width), (locals_, edges), (3 * slots, edges)],
        [*firsts[1:], firsts[0], onehot, mask, inc, capacity, dual_start], flops=flops,
    )
    dual_shape, term_shape = (locals_, edges), (incs, width)
    (turned_inc,) = kernel_call(
        turn_kernel, "transpose", [jax.ShapeDtypeStruct((incs, edges, width), half)], [tied(inc, out)]
    )
    limit, duals, terms = kernel_call(
        lambda *refs: first_dual_kernel(others, unit, *refs), "first_duals",
        [dual_shape, dual_shape, term_shape],
        [*trade(out), choice, load, capacity, dual_start, mask, turned_inc], flops=flops,
    )
    for iteration in range(ITERS):
        near = share(terms, stages[:-1])
        if iteration == 0:
            (limits,) = kernel_call(
                lambda *refs: pick_kernel(len(firsts), blocks, *refs), "pick", [(rows, width)],
                [*firsts, onehot],
            )
        (part,) = kernel_call(
            part_kernel, "own_sums", [(far_count * rows, width)], [terms, *utilities, own_same]
        )
        if near[0].shape == terms.shape:
            near, skip = near[1:], 0
        else:
            skip = incs
        sums = kernel_call(
            lambda *refs: sum_kernel(len(near), skip, *refs), "sums", [(rows, width)] * far_count,
            [*near, other_same, part],
        )
        far = [sums[0]] + [
            lax.ppermute(x, "shard", [(i, i ^ (k * stride)) for i in range(devices)])
            for k, x in enumerate(sums) if k > 0
        ]
        flows, load, out = kernel_call(
            lambda *refs: flow_kernel(len(far), step_size, *refs), "flows", load_shapes,
            [far[2], far[3], far[1], far[0], flows, limits, mask, inc], flops=flops,
        )
        operands = [*trade(out), choice, load, limit, duals]
        if iteration < ITERS - 1:
            duals, terms = kernel_call(
                lambda *refs: dual_kernel(others, *refs), "duals", [dual_shape, term_shape],
                [*operands, mask, turned_inc], flops=flops,
            )
    (duals,) = kernel_call(
        lambda *refs: last_dual_kernel(others, *refs), "last_duals", [dual_shape], operands
    )
    return flows[incs:], duals


def solution(mesh):
    whole = P(("cluster", "shard"))
    wide = P(("cluster", "shard"), None)
    return jax.shard_map(
        body,
        mesh=mesh,
        in_specs=(
            wide, wide, wide, whole, P("cluster"), P(("cluster", "shard"), None, None),
            whole, whole, wide, wide, P("cluster", None),
        ),
        out_specs=(wide, wide),
        check_vma=False,
    )
```

```python
import jax
import jax.numpy as jnp
from jax import lax
from jax.experimental import pallas as pl
from jax.experimental.pallas import tpu as pltpu
from jax.sharding import PartitionSpec as P

ITERS = 3
SUB = 8
VMEM = pl.BlockSpec(memory_space=pltpu.VMEM)


def split3(x):
    high = x.astype(jnp.bfloat16)
    rest = x - high.astype(jnp.float32)
    middle = rest.astype(jnp.bfloat16)
    low = (rest - middle.astype(jnp.float32)).astype(jnp.bfloat16)
    return high, middle, low


def column_of(row):
    n = row.shape[1]
    down = lax.broadcasted_iota(jnp.int32, (n, n), 0)
    along = lax.broadcasted_iota(jnp.int32, (n, n), 1)
    return jnp.sum(jnp.where(down == along, row, 0.0), axis=1, keepdims=True)


def pick_thrice(thrice, rows):
    parts = jnp.concatenate(split3(rows), axis=0)
    return jnp.dot(thrice, parts, preferred_element_type=jnp.float32)


def copy_all(pairs, sems):
    copies = [pltpu.make_async_copy(*pair, sems.at[k]) for k, pair in enumerate(pairs)]
    for copy in copies:
        copy.start()
    for copy in copies:
        copy.wait()


def prep_kernel(
    start_hbm, demand_hbm, utility_hbm, path_hbm, count_hbm, size_hbm,
    first_ref, start_ref, demand_ref, path_ref, count_ref, size_ref, sems,
):
    blocks, width = start_ref.shape
    incs = path_ref.shape[1]
    copy_all(
        [
            (start_hbm, start_ref),
            (demand_hbm, demand_ref),
            (utility_hbm, first_ref.at[2 * blocks + SUB :]),
            (path_hbm, path_ref),
            (count_hbm, count_ref),
            (size_hbm, size_ref),
        ],
        sems,
    )
    lanes = lax.broadcasted_iota(jnp.int32, (1, width), 1)
    limits = []
    for j in range(blocks):
        count = jnp.where(j < size_ref[0], count_ref[j], 0)
        limits.append(jnp.where(lanes < count, demand_ref[j : j + 1, :], 0.0))
    limit = jnp.concatenate(limits, axis=0)
    first_ref[:blocks] = jnp.minimum(jnp.maximum(start_ref[...], 0.0), limit)
    first_ref[blocks : 2 * blocks] = limit
    first_ref[2 * blocks : 2 * blocks + SUB] = jnp.zeros((SUB, width), jnp.float32)
    first_ref[2 * blocks : 2 * blocks + 1, :incs] = path_ref[...].astype(jnp.float32)


def table_kernel(
    path_hbm, edge_hbm, partner_hbm,
    onehot_ref, mask_ref, choice_ref, path_ref, edge_ref, partner_ref, sems,
):
    incs = path_ref.shape[1]
    blocks = onehot_ref.shape[0] - incs
    cluster, shard = lax.axis_index("cluster"), lax.axis_index("shard")
    copy_all([(path_hbm, path_ref), (edge_hbm, edge_ref), (partner_hbm, partner_ref)], sems)
    names = path_ref[...]
    place = jnp.bitwise_xor(names // blocks, shard) * blocks + names % blocks
    total = onehot_ref.shape[1] // 3
    along = lax.broadcasted_iota(jnp.int32, (incs, total), 1).astype(jnp.float32)
    picked = jnp.where(along == column_of(place.astype(jnp.float32)), 1.0, 0.0)
    down = lax.broadcasted_iota(jnp.int32, (blocks, total), 0)
    own = jnp.where(down == lax.broadcasted_iota(jnp.int32, (blocks, total), 1), 1.0, 0.0)
    once = jnp.concatenate([picked, own], axis=0)
    onehot_ref[...] = jnp.concatenate([once] * 3, axis=1).astype(jnp.bfloat16)
    edge = lax.broadcasted_iota(jnp.int32, mask_ref.shape, 0)
    mask_ref[...] = jnp.where(edge == edge_ref[...], 1.0, 0.0)
    for k in range(choice_ref.shape[0]):
        for j in range(partner_ref.shape[1]):
            chosen = jnp.where(partner_ref[0, j] == jnp.bitwise_xor(cluster, k + 1), 1.0, 0.0)
            choice_ref[k, j : j + 1, :] = jnp.full((1, choice_ref.shape[2]), chosen, jnp.float32)


def cast_kernel(inc_ref, out_ref):
    out_ref[...] = inc_ref[...].astype(jnp.bfloat16)


def turn_kernel(inc_ref, out_ref):
    for i in range(inc_ref.shape[0]):
        out_ref[i] = inc_ref[i].T


def load_of(flows, mask, inc_ref):
    count, width, edges = inc_ref.shape
    parts = [p.astype(jnp.float32) for p in split3(flows)]
    rest = jnp.zeros((SUB - len(parts), width), jnp.float32)
    load = jnp.zeros((SUB, edges), jnp.float32)
    for i in range(count):
        rows = jnp.concatenate([*[p[i : i + 1] for p in parts], rest], axis=0)
        got = jnp.dot(rows.astype(jnp.bfloat16), inc_ref[i], preferred_element_type=jnp.float32)
        load += mask[:, i : i + 1] * jnp.sum(got, axis=0, keepdims=True)
    return load


def put_load(load, load_ref, border_ref):
    slots = border_ref.shape[0]
    interior = load_ref.shape[0] - slots
    load_ref[...] = load[: load_ref.shape[0]]
    border_ref[...] = load[interior : interior + slots]


def offsets(ref, blocks):
    return [0, *range(2 * blocks + SUB, ref.shape[0], 2 * blocks)]


def start_kernel(pieces, *refs):
    ins, (onehot_ref, mask_ref, inc_ref, cap_ref, dual_ref, flows_ref, load_ref, border_ref) = refs[:pieces], refs[pieces:]
    incs = inc_ref.shape[0]
    ins = [ins[-1], *ins[:-1]]
    blocks = flows_ref.shape[0] - incs
    rows = [ref[k : k + blocks] for ref in ins for k in offsets(ref, blocks)]
    flows = pick_thrice(onehot_ref[...], jnp.concatenate(rows, axis=0))
    flows_ref[...] = flows
    slots = border_ref.shape[0] // 3
    interior = cap_ref.shape[0] - slots
    put_load(load_of(flows[:incs], mask_ref[...], inc_ref), load_ref, border_ref.at[:slots])
    border_ref[slots : 2 * slots] = cap_ref[interior:]
    border_ref[2 * slots :] = dual_ref[interior:]


def pick_kernel(pieces, blocks, *refs):
    ins, (onehot_ref, limit_ref) = refs[:pieces], refs[pieces:]
    rows = [ref[k + blocks : k + 2 * blocks] for ref in ins for k in offsets(ref, blocks)]
    limit_ref[...] = pick_thrice(onehot_ref[...], jnp.concatenate(rows, axis=0))


def relate_kernel(pieces, blocks, incs, stride, *refs):
    ins, near, (own_ref, others_ref) = refs[:pieces], refs[pieces:-2], refs[-2:]
    rows = incs + blocks
    shard = lax.axis_index("shard")
    at = 2 * blocks
    group = 3 * blocks + SUB
    names = [ref[k : k + 1, :incs] for ref in near for k in range(at, ref.shape[0], group)]
    along = lax.broadcasted_iota(jnp.int32, (1, blocks), 1)
    owned = [
        (along + jnp.bitwise_xor(shard, k) * blocks).astype(jnp.float32) for k in range(stride)
    ]
    others = jnp.concatenate(names[1:] * 3, axis=1)
    here = jnp.concatenate([names[0], *owned] * 3, axis=1)
    column = lax.broadcasted_iota(jnp.int32, here.shape, 1) % (incs + stride * blocks)
    weight = jnp.where(column < incs, 1.0, -1.0)
    down = lax.broadcasted_iota(jnp.int32, (blocks, 1), 0)
    for k, ref in enumerate(ins):
        own = (down + jnp.bitwise_xor(shard, k * stride) * blocks).astype(jnp.float32)
        wanted = column_of(ref[2 * blocks : 2 * blocks + 1, :incs])
        wanted = jnp.concatenate([wanted, own], axis=0)
        place = slice(k * rows, (k + 1) * rows)
        own_ref[place] = jnp.where(wanted == here, weight, 0.0).astype(jnp.bfloat16)
        others_ref[place] = jnp.where(wanted == others, 1.0, 0.0).astype(jnp.bfloat16)


def part_kernel(terms_ref, *refs):
    ins, (own_ref, out_ref) = refs[:-2], refs[-2:]
    rows = jnp.concatenate([terms_ref[...], *[ref[...] for ref in ins]], axis=0)
    out_ref[...] = pick_thrice(own_ref[...], rows)


def sum_kernel(pieces, skip, *refs):
    ins, (others_ref, part_ref), outs = refs[:pieces], refs[pieces : pieces + 2], refs[pieces + 2 :]
    terms = jnp.concatenate([ref[...] for ref in ins], axis=0)[skip:]
    total = part_ref[...] + pick_thrice(others_ref[...], terms)
    rows = outs[0].shape[0]
    for k, out in enumerate(outs):
        out[...] = total[k * rows : (k + 1) * rows]


def flow_kernel(pieces, step_size, *refs):
    ins = refs[:pieces]
    flows_ref, limit_ref, mask_ref, inc_ref, out_ref, load_ref, border_ref = refs[pieces:]
    slope = ins[0][...]
    for ref in ins[1:]:
        slope += ref[...]
    flows = flows_ref[...] - step_size * slope
    flows = jnp.minimum(jnp.maximum(flows, 0.0), limit_ref[...])
    out_ref[...] = flows
    put_load(load_of(flows[: inc_ref.shape[0]], mask_ref[...], inc_ref), load_ref, border_ref)


def twin_of(ins, choice_ref):
    total = None
    for k, ref in enumerate(ins):
        term = jnp.where(choice_ref[k] > 0.5, ref[...], 0.0)
        total = term if total is None else total + term
    return total


def settle(ins, choice_ref, load_ref, limit, duals):
    load = load_ref[...]
    slots = ins[0].shape[0]
    interior = load.shape[0] - slots
    load = jnp.concatenate([load[:interior], load[interior:] + twin_of(ins, choice_ref)], axis=0)
    split = jnp.minimum(limit, load + duals)
    duals = (duals + load) - split
    return (load - split) + duals, duals


def back_terms(residual, mask, inc_ref, out_ref):
    rows = residual.shape[0]
    if rows < SUB:
        residual = jnp.concatenate(
            [residual, jnp.zeros((SUB - rows, residual.shape[1]), jnp.float32)], axis=0
        )
    parts = [p.astype(jnp.float32) for p in split3(residual)]
    left = jnp.concatenate(parts, axis=0).astype(jnp.bfloat16)
    for i in range(inc_ref.shape[0]):
        got = jnp.dot(left, inc_ref[i], preferred_element_type=jnp.float32)
        got = got[:SUB] + got[SUB : 2 * SUB] + got[2 * SUB :]
        out_ref[i : i + 1, :] = jnp.sum(got * mask[:, i : i + 1], axis=0, keepdims=True)


def first_dual_kernel(others, unit, *refs):
    ins = refs[:others]
    (choice_ref, load_ref, cap_ref, dual_ref, mask_ref, inc_ref,
     limit_ref, out_ref, terms_ref) = refs[others:]
    slots = ins[0].shape[0] // 3
    interior = load_ref.shape[0] - slots
    loads, caps, starts = [[r.at[k * slots : (k + 1) * slots] for r in ins] for k in range(3)]

    def shared(ref, twins):
        mean = 0.5 * (ref[interior:] + twin_of(twins, choice_ref))
        return jnp.concatenate([ref[:interior], mean], axis=0)

    limit = unit * shared(cap_ref, caps)
    limit_ref[...] = limit
    residual, duals = settle(loads, choice_ref, load_ref, limit, shared(dual_ref, starts))
    out_ref[...] = duals
    back_terms(residual, mask_ref[...], inc_ref, terms_ref)


def dual_kernel(others, *refs):
    ins = refs[:others]
    (choice_ref, load_ref, limit_ref, dual_ref, mask_ref, inc_ref,
     out_ref, terms_ref) = refs[others:]
    residual, duals = settle(ins, choice_ref, load_ref, limit_ref[...], dual_ref[...])
    out_ref[...] = duals
    back_terms(residual, mask_ref[...], inc_ref, terms_ref)


def last_dual_kernel(others, *refs):
    ins = refs[:others]
    choice_ref, load_ref, limit_ref, dual_ref, out_ref = refs[others:]
    out_ref[...] = settle(ins, choice_ref, load_ref, limit_ref[...], dual_ref[...])[1]


def kernel_call(kernel, name, outs, operands, flops=0, scratch=(), pin=False):
    shapes = tuple(x if hasattr(x, "dtype") else jax.ShapeDtypeStruct(x, jnp.float32) for x in outs)
    size = sum(x.size * x.dtype.itemsize for x in operands)
    if pin:
        operands = [pltpu.with_memory_space_constraint(x, pltpu.HBM) if x.size > 1 else x for x in operands]
    return pl.pallas_call(
        kernel,
        out_shape=shapes,
        in_specs=[pl.BlockSpec(memory_space=pltpu.HBM if pin else pltpu.VMEM)] * len(operands),
        out_specs=tuple(VMEM for _ in outs),
        scratch_shapes=scratch,
        compiler_params=pltpu.CompilerParams(vmem_limit_bytes=16 * 1024 * 1024),
        cost_estimate=pl.CostEstimate(flops=flops, bytes_accessed=size, transcendentals=0),
        name=name,
    )(*operands)


def body(
    flow_start,
    demand,
    utility,
    path_count,
    cluster_size,
    incidence,
    inc_path,
    inc_edge,
    capacity,
    dual_start,
    partner,
):
    blocks, width = flow_start.shape
    incs = incidence.shape[0]
    edges = incidence.shape[2]
    locals_ = capacity.shape[0]
    slots = partner.shape[1]
    clusters, devices = lax.axis_size("cluster"), lax.axis_size("shard")
    cluster, shard = lax.axis_index("cluster"), lax.axis_index("shard")
    rows = incs + blocks
    norm_bound = max(2, incs * incs * width * edges // (1024 * locals_ * blocks))
    unit = float(max(1, incs * width // (160 * locals_)))
    step_size = 1.0 / (2.0 * norm_bound)
    bits = devices.bit_length() - 1
    assert devices == 1 << bits and clusters & (clusters - 1) == 0
    stages = [1] * (bits % 2) + [2] * (bits // 2)

    def share(x, stages, shift=0, hold=None):
        pieces = x if isinstance(x, list) else [x]
        for step in stages:
            now = pieces[0] if len(pieces) == 1 else jnp.concatenate(pieces, axis=0)
            pieces = [now]
            for k in range(1, 1 << step):
                pairs = [(i, i ^ (k << shift)) for i in range(devices)]
                given = now if hold is None else tied(now, hold[min(len(hold), (1 << step) - k) - 1])
                pieces.append(lax.ppermute(given, "shard", pairs))
            shift += step
        return pieces

    def trade(x):
        return [
            lax.ppermute(x, "cluster", [(i, i ^ k) for i in range(clusters)])
            for k in range(1, clusters)
        ]

    def tied(x, *after):
        return lax.optimization_barrier((x, *after))[0]

    stages_first, stages_rest = stages[:1], stages[1:]
    half = jnp.bfloat16
    (first,) = kernel_call(
        prep_kernel,
        "prepare",
        [(3 * blocks + SUB, width)],
        [flow_start, demand, utility, inc_path[None, :], path_count, cluster_size],
        scratch=[
            pltpu.VMEM((blocks, width), jnp.float32),
            pltpu.VMEM((blocks, width), jnp.float32),
            pltpu.VMEM((1, incs), jnp.int32),
            pltpu.SMEM((blocks,), jnp.int32),
            pltpu.SMEM((1,), jnp.int32),
            pltpu.SemaphoreType.DMA((6,)),
        ],
        pin=True,
    )
    onehot, mask, choice = kernel_call(
        table_kernel,
        "tables",
        [
            jax.ShapeDtypeStruct((rows, 3 * blocks * devices), half),
            (SUB, incs),
            (clusters - 1, slots, edges),
        ],
        [tied(inc_path, first)[None, :], inc_edge[None, :], partner],
        scratch=[
            pltpu.VMEM((1, incs), jnp.int32),
            pltpu.VMEM((1, incs), jnp.int32),
            pltpu.SMEM((1, slots), jnp.int32),
            pltpu.SemaphoreType.DMA((3,)),
        ],
        pin=True,
    )

    limits_end, kept = 2 * blocks, 2 * blocks + SUB
    near_firsts = share(first, stages[:-1])
    groups = [p[k : k + kept + blocks] for p in near_firsts for k in range(0, p.shape[0], kept + blocks)]
    utilities = [p[kept:] for p in groups]
    firsts = [jnp.concatenate([groups[0][:kept], *[p[:limits_end] for p in groups[1:]]], axis=0)]
    inc = pl.pallas_call(
        cast_kernel,
        grid=(4,),
        in_specs=[pl.BlockSpec((incs // 4, width, edges), lambda k: (k, 0, 0))],
        out_specs=pl.BlockSpec((incs // 4, width, edges), lambda k: (k, 0, 0)),
        out_shape=jax.ShapeDtypeStruct(incidence.shape, half),
        compiler_params=pltpu.CompilerParams(vmem_limit_bytes=16 * 1024 * 1024),
        cost_estimate=pl.CostEstimate(flops=0, bytes_accessed=6 * incidence.size, transcendentals=0),
        name="cast",
    )(tied(incidence, firsts[-1]))
    firsts = [tied(firsts[0], onehot)]
    firsts = share(firsts, stages[-1:], bits - stages[-1])
    far_count, stride = 1 << stages[-1], devices >> stages[-1]
    own_same, other_same = kernel_call(
        lambda *refs: relate_kernel(far_count, blocks, incs, stride, *refs), "relate",
        [
            jax.ShapeDtypeStruct((far_count * rows, 3 * (incs + stride * blocks)), half),
            jax.ShapeDtypeStruct((far_count * rows, 3 * incs * (stride - 1)), half),
        ],
        [*firsts, *near_firsts],
    )

    others = clusters - 1
    flops = 2 * incs * width * edges * SUB
    load_shapes = [(rows, width), (locals_, edges), (slots, edges)]
    flows, load, out = kernel_call(
        lambda *refs: start_kernel(len(firsts), *refs), "first_load",
        [(rows, width), (locals_, edges), (3 * slots, edges)],
        [*firsts[1:], firsts[0], onehot, mask, inc, capacity, dual_start], flops=flops,
    )
    dual_shape, term_shape = (locals_, edges), (incs, width)
    (turned_inc,) = kernel_call(
        turn_kernel, "transpose", [jax.ShapeDtypeStruct((incs, edges, width), half)], [tied(inc, out)]
    )
    limit, duals, terms = kernel_call(
        lambda *refs: first_dual_kernel(others, unit, *refs), "first_duals",
        [dual_shape, dual_shape, term_shape],
        [*trade(out), choice, load, capacity, dual_start, mask, turned_inc], flops=flops,
    )
    for iteration in range(ITERS):
        near = share(terms, stages[:-1])
        if iteration == 0:
            (limits,) = kernel_call(
                lambda *refs: pick_kernel(len(firsts), blocks, *refs), "pick", [(rows, width)],
                [*firsts, onehot],
            )
        (part,) = kernel_call(
            part_kernel, "own_sums", [(far_count * rows, width)], [terms, *utilities, own_same]
        )
        if near[0].shape == terms.shape:
            near, skip = near[1:], 0
        else:
            skip = incs
        sums = kernel_call(
            lambda *refs: sum_kernel(len(near), skip, *refs), "sums", [(rows, width)] * far_count,
            [*near, other_same, part],
        )
        far = [sums[0]] + [
            lax.ppermute(x, "shard", [(i, i ^ (k * stride)) for i in range(devices)])
            for k, x in enumerate(sums) if k > 0
        ]
        flows, load, out = kernel_call(
            lambda *refs: flow_kernel(len(far), step_size, *refs), "flows", load_shapes,
            [far[2], far[3], far[1], far[0], flows, limits, mask, inc], flops=flops,
        )
        operands = [*trade(out), choice, load, limit, duals]
        if iteration < ITERS - 1:
            duals, terms = kernel_call(
                lambda *refs: dual_kernel(others, *refs), "duals", [dual_shape, term_shape],
                [*operands, mask, turned_inc], flops=flops,
            )
    (duals,) = kernel_call(
        lambda *refs: last_dual_kernel(others, *refs), "last_duals", [dual_shape], operands
    )
    return flows[incs:], duals


def solution(mesh):
    whole = P(("cluster", "shard"))
    wide = P(("cluster", "shard"), None)
    return jax.shard_map(
        body,
        mesh=mesh,
        in_specs=(
            wide, wide, wide, whole, P("cluster"), P(("cluster", "shard"), None, None),
            whole, whole, wide, wide, P("cluster", None),
        ),
        out_specs=(wide, wide),
        check_vma=False,
    )
```

```python
import jax
import jax.numpy as jnp
from jax import lax
from jax.experimental import pallas as pl
from jax.experimental.pallas import tpu as pltpu
from jax.sharding import PartitionSpec as P

ITERS = 3
SUB = 8
VMEM = pl.BlockSpec(memory_space=pltpu.VMEM)


def split3(x):
    high = x.astype(jnp.bfloat16)
    rest = x - high.astype(jnp.float32)
    middle = rest.astype(jnp.bfloat16)
    low = (rest - middle.astype(jnp.float32)).astype(jnp.bfloat16)
    return high, middle, low


def column_of(row):
    n = row.shape[1]
    down = lax.broadcasted_iota(jnp.int32, (n, n), 0)
    along = lax.broadcasted_iota(jnp.int32, (n, n), 1)
    return jnp.sum(jnp.where(down == along, row, 0.0), axis=1, keepdims=True)


def pick_thrice(thrice, rows):
    parts = jnp.concatenate(split3(rows), axis=0)
    return jnp.dot(thrice, parts, preferred_element_type=jnp.float32)


def copy_all(pairs, sems):
    copies = [pltpu.make_async_copy(*pair, sems.at[k]) for k, pair in enumerate(pairs)]
    for copy in copies:
        copy.start()
    for copy in copies:
        copy.wait()


def prep_kernel(
    start_hbm, demand_hbm, utility_hbm, path_hbm, count_hbm, size_hbm,
    first_ref, start_ref, demand_ref, path_ref, count_ref, size_ref, sems,
):
    blocks, width = start_ref.shape
    incs = path_ref.shape[1]
    copy_all(
        [
            (start_hbm, start_ref),
            (demand_hbm, demand_ref),
            (utility_hbm, first_ref.at[2 * blocks + SUB :]),
            (path_hbm, path_ref),
            (count_hbm, count_ref),
            (size_hbm, size_ref),
        ],
        sems,
    )
    lanes = lax.broadcasted_iota(jnp.int32, (1, width), 1)
    limits = []
    for j in range(blocks):
        count = jnp.where(j < size_ref[0], count_ref[j], 0)
        limits.append(jnp.where(lanes < count, demand_ref[j : j + 1, :], 0.0))
    limit = jnp.concatenate(limits, axis=0)
    first_ref[:blocks] = jnp.minimum(jnp.maximum(start_ref[...], 0.0), limit)
    first_ref[blocks : 2 * blocks] = limit
    first_ref[2 * blocks : 2 * blocks + SUB] = jnp.zeros((SUB, width), jnp.float32)
    first_ref[2 * blocks : 2 * blocks + 1, :incs] = path_ref[...].astype(jnp.float32)


def table_kernel(
    path_hbm, edge_hbm, partner_hbm,
    onehot_ref, mask_ref, choice_ref, path_ref, edge_ref, partner_ref, sems,
):
    incs = path_ref.shape[1]
    blocks = onehot_ref.shape[0] - incs
    cluster, shard = lax.axis_index("cluster"), lax.axis_index("shard")
    copy_all([(path_hbm, path_ref), (edge_hbm, edge_ref), (partner_hbm, partner_ref)], sems)
    names = path_ref[...]
    place = jnp.bitwise_xor(names // blocks, shard) * blocks + names % blocks
    total = onehot_ref.shape[1] // 3
    along = lax.broadcasted_iota(jnp.int32, (incs, total), 1).astype(jnp.float32)
    picked = jnp.where(along == column_of(place.astype(jnp.float32)), 1.0, 0.0)
    down = lax.broadcasted_iota(jnp.int32, (blocks, total), 0)
    own = jnp.where(down == lax.broadcasted_iota(jnp.int32, (blocks, total), 1), 1.0, 0.0)
    once = jnp.concatenate([picked, own], axis=0)
    onehot_ref[...] = jnp.concatenate([once] * 3, axis=1).astype(jnp.bfloat16)
    edge = lax.broadcasted_iota(jnp.int32, mask_ref.shape, 0)
    mask_ref[...] = jnp.where(edge == edge_ref[...], 1.0, 0.0)
    for k in range(choice_ref.shape[0]):
        for j in range(partner_ref.shape[1]):
            chosen = jnp.where(partner_ref[0, j] == jnp.bitwise_xor(cluster, k + 1), 1.0, 0.0)
            choice_ref[k, j : j + 1, :] = jnp.full((1, choice_ref.shape[2]), chosen, jnp.float32)


def cast_kernel(inc_ref, out_ref):
    out_ref[...] = inc_ref[...].astype(jnp.bfloat16)


def turn_kernel(inc_ref, out_ref):
    for i in range(inc_ref.shape[0]):
        out_ref[i] = inc_ref[i].T


def load_of(flows, mask, inc_ref):
    count, width, edges = inc_ref.shape
    parts = [p.astype(jnp.float32) for p in split3(flows)]
    rest = jnp.zeros((SUB - len(parts), width), jnp.float32)
    load = jnp.zeros((SUB, edges), jnp.float32)
    for i in range(count):
        rows = jnp.concatenate([*[p[i : i + 1] for p in parts], rest], axis=0)
        got = jnp.dot(rows.astype(jnp.bfloat16), inc_ref[i], preferred_element_type=jnp.float32)
        load += mask[:, i : i + 1] * jnp.sum(got, axis=0, keepdims=True)
    return load


def put_load(load, load_ref, border_ref):
    slots = border_ref.shape[0]
    interior = load_ref.shape[0] - slots
    load_ref[...] = load[: load_ref.shape[0]]
    border_ref[...] = load[interior : interior + slots]


def offsets(ref, blocks):
    return [0, *range(2 * blocks + SUB, ref.shape[0], 2 * blocks)]


def start_kernel(pieces, *refs):
    ins, (onehot_ref, mask_ref, inc_ref, cap_ref, dual_ref, flows_ref, load_ref, border_ref) = refs[:pieces], refs[pieces:]
    incs = inc_ref.shape[0]
    ins = [ins[-1], *ins[:-1]]
    blocks = flows_ref.shape[0] - incs
    rows = [ref[k : k + blocks] for ref in ins for k in offsets(ref, blocks)]
    flows = pick_thrice(onehot_ref[...], jnp.concatenate(rows, axis=0))
    flows_ref[...] = flows
    slots = border_ref.shape[0] // 3
    interior = cap_ref.shape[0] - slots
    put_load(load_of(flows[:incs], mask_ref[...], inc_ref), load_ref, border_ref.at[:slots])
    border_ref[slots : 2 * slots] = cap_ref[interior:]
    border_ref[2 * slots :] = dual_ref[interior:]


def pick_kernel(pieces, blocks, *refs):
    ins, (onehot_ref, limit_ref) = refs[:pieces], refs[pieces:]
    rows = [ref[k + blocks : k + 2 * blocks] for ref in ins for k in offsets(ref, blocks)]
    limit_ref[...] = pick_thrice(onehot_ref[...], jnp.concatenate(rows, axis=0))


def relate_kernel(pieces, blocks, incs, stride, *refs):
    ins, near, (own_ref, others_ref) = refs[:pieces], refs[pieces:-2], refs[-2:]
    rows = incs + blocks
    shard = lax.axis_index("shard")
    at = 2 * blocks
    group = 3 * blocks + SUB
    names = [ref[k : k + 1, :incs] for ref in near for k in range(at, ref.shape[0], group)]
    along = lax.broadcasted_iota(jnp.int32, (1, blocks), 1)
    owned = [
        (along + jnp.bitwise_xor(shard, k) * blocks).astype(jnp.float32) for k in range(stride)
    ]
    others = jnp.concatenate(names[1:] * 3, axis=1)
    here = jnp.concatenate([names[0], *owned] * 3, axis=1)
    column = lax.broadcasted_iota(jnp.int32, here.shape, 1) % (incs + stride * blocks)
    weight = jnp.where(column < incs, 1.0, -1.0)
    down = lax.broadcasted_iota(jnp.int32, (blocks, 1), 0)
    for k, ref in enumerate(ins):
        own = (down + jnp.bitwise_xor(shard, k * stride) * blocks).astype(jnp.float32)
        wanted = column_of(ref[2 * blocks : 2 * blocks + 1, :incs])
        wanted = jnp.concatenate([wanted, own], axis=0)
        place = slice(k * rows, (k + 1) * rows)
        own_ref[place] = jnp.where(wanted == here, weight, 0.0).astype(jnp.bfloat16)
        others_ref[place] = jnp.where(wanted == others, 1.0, 0.0).astype(jnp.bfloat16)


def part_kernel(terms_ref, *refs):
    ins, (own_ref, out_ref) = refs[:-2], refs[-2:]
    rows = jnp.concatenate([terms_ref[...], *[ref[...] for ref in ins]], axis=0)
    out_ref[...] = pick_thrice(own_ref[...], rows)


def sum_kernel(pieces, skip, first, *refs):
    ins, (others_ref, part_ref), outs = refs[:pieces], refs[pieces : pieces + 2], refs[pieces + 2 :]
    terms = jnp.concatenate([ref[...] for ref in ins], axis=0)[skip:]
    rows = outs[0].shape[0]
    place = slice(first * rows, (first + len(outs)) * rows)
    total = part_ref[place] + pick_thrice(others_ref[place], terms)
    for k, out in enumerate(outs):
        out[...] = total[k * rows : (k + 1) * rows]


def flow_kernel(pieces, step_size, *refs):
    ins = refs[:pieces]
    flows_ref, limit_ref, mask_ref, inc_ref, out_ref, load_ref, border_ref = refs[pieces:]
    slope = ins[0][...]
    for ref in ins[1:]:
        slope += ref[...]
    flows = flows_ref[...] - step_size * slope
    flows = jnp.minimum(jnp.maximum(flows, 0.0), limit_ref[...])
    out_ref[...] = flows
    put_load(load_of(flows[: inc_ref.shape[0]], mask_ref[...], inc_ref), load_ref, border_ref)


def twin_of(ins, choice_ref):
    total = None
    for k, ref in enumerate(ins):
        term = jnp.where(choice_ref[k] > 0.5, ref[...], 0.0)
        total = term if total is None else total + term
    return total


def settle(ins, choice_ref, load_ref, limit, duals):
    load = load_ref[...]
    slots = ins[0].shape[0]
    interior = load.shape[0] - slots
    load = jnp.concatenate([load[:interior], load[interior:] + twin_of(ins, choice_ref)], axis=0)
    split = jnp.minimum(limit, load + duals)
    duals = (duals + load) - split
    return (load - split) + duals, duals


def back_terms(residual, mask, inc_ref, out_ref):
    rows = residual.shape[0]
    if rows < SUB:
        residual = jnp.concatenate(
            [residual, jnp.zeros((SUB - rows, residual.shape[1]), jnp.float32)], axis=0
        )
    parts = [p.astype(jnp.float32) for p in split3(residual)]
    left = jnp.concatenate(parts, axis=0).astype(jnp.bfloat16)
    for i in range(inc_ref.shape[0]):
        got = jnp.dot(left, inc_ref[i], preferred_element_type=jnp.float32)
        got = got[:SUB] + got[SUB : 2 * SUB] + got[2 * SUB :]
        out_ref[i : i + 1, :] = jnp.sum(got * mask[:, i : i + 1], axis=0, keepdims=True)


def first_dual_kernel(others, unit, *refs):
    ins = refs[:others]
    (choice_ref, load_ref, cap_ref, dual_ref, mask_ref, inc_ref,
     limit_ref, out_ref, terms_ref) = refs[others:]
    slots = ins[0].shape[0] // 3
    interior = load_ref.shape[0] - slots
    loads, caps, starts = [[r.at[k * slots : (k + 1) * slots] for r in ins] for k in range(3)]

    def shared(ref, twins):
        mean = 0.5 * (ref[interior:] + twin_of(twins, choice_ref))
        return jnp.concatenate([ref[:interior], mean], axis=0)

    limit = unit * shared(cap_ref, caps)
    limit_ref[...] = limit
    residual, duals = settle(loads, choice_ref, load_ref, limit, shared(dual_ref, starts))
    out_ref[...] = duals
    back_terms(residual, mask_ref[...], inc_ref, terms_ref)


def dual_kernel(others, *refs):
    ins = refs[:others]
    (choice_ref, load_ref, limit_ref, dual_ref, mask_ref, inc_ref,
     out_ref, terms_ref) = refs[others:]
    residual, duals = settle(ins, choice_ref, load_ref, limit_ref[...], dual_ref[...])
    out_ref[...] = duals
    back_terms(residual, mask_ref[...], inc_ref, terms_ref)


def last_dual_kernel(others, *refs):
    ins = refs[:others]
    choice_ref, load_ref, limit_ref, dual_ref, out_ref = refs[others:]
    out_ref[...] = settle(ins, choice_ref, load_ref, limit_ref[...], dual_ref[...])[1]


def kernel_call(kernel, name, outs, operands, flops=0, scratch=(), pin=False):
    shapes = tuple(x if hasattr(x, "dtype") else jax.ShapeDtypeStruct(x, jnp.float32) for x in outs)
    size = sum(x.size * x.dtype.itemsize for x in operands)
    if pin:
        operands = [pltpu.with_memory_space_constraint(x, pltpu.HBM) if x.size > 1 else x for x in operands]
    return pl.pallas_call(
        kernel,
        out_shape=shapes,
        in_specs=[pl.BlockSpec(memory_space=pltpu.HBM if pin else pltpu.VMEM)] * len(operands),
        out_specs=tuple(VMEM for _ in outs),
        scratch_shapes=scratch,
        compiler_params=pltpu.CompilerParams(vmem_limit_bytes=16 * 1024 * 1024),
        cost_estimate=pl.CostEstimate(flops=flops, bytes_accessed=size, transcendentals=0),
        name=name,
    )(*operands)


def body(
    flow_start,
    demand,
    utility,
    path_count,
    cluster_size,
    incidence,
    inc_path,
    inc_edge,
    capacity,
    dual_start,
    partner,
):
    blocks, width = flow_start.shape
    incs = incidence.shape[0]
    edges = incidence.shape[2]
    locals_ = capacity.shape[0]
    slots = partner.shape[1]
    clusters, devices = lax.axis_size("cluster"), lax.axis_size("shard")
    cluster, shard = lax.axis_index("cluster"), lax.axis_index("shard")
    rows = incs + blocks
    norm_bound = max(2, incs * incs * width * edges // (1024 * locals_ * blocks))
    unit = float(max(1, incs * width // (160 * locals_)))
    step_size = 1.0 / (2.0 * norm_bound)
    bits = devices.bit_length() - 1
    assert devices == 1 << bits and clusters & (clusters - 1) == 0
    stages = [1] * (bits % 2) + [2] * (bits // 2)

    def share(x, stages, shift=0, hold=None):
        pieces = x if isinstance(x, list) else [x]
        for step in stages:
            now = pieces[0] if len(pieces) == 1 else jnp.concatenate(pieces, axis=0)
            pieces = [now]
            for k in range(1, 1 << step):
                pairs = [(i, i ^ (k << shift)) for i in range(devices)]
                given = now if hold is None else tied(now, hold[min(len(hold), (1 << step) - k) - 1])
                pieces.append(lax.ppermute(given, "shard", pairs))
            shift += step
        return pieces

    def trade(x):
        return [
            lax.ppermute(x, "cluster", [(i, i ^ k) for i in range(clusters)])
            for k in range(1, clusters)
        ]

    def tied(x, *after):
        return lax.optimization_barrier((x, *after))[0]

    stages_first, stages_rest = stages[:1], stages[1:]
    half = jnp.bfloat16
    (first,) = kernel_call(
        prep_kernel,
        "prepare",
        [(3 * blocks + SUB, width)],
        [flow_start, demand, utility, inc_path[None, :], path_count, cluster_size],
        scratch=[
            pltpu.VMEM((blocks, width), jnp.float32),
            pltpu.VMEM((blocks, width), jnp.float32),
            pltpu.VMEM((1, incs), jnp.int32),
            pltpu.SMEM((blocks,), jnp.int32),
            pltpu.SMEM((1,), jnp.int32),
            pltpu.SemaphoreType.DMA((6,)),
        ],
        pin=True,
    )
    onehot, mask, choice = kernel_call(
        table_kernel,
        "tables",
        [
            jax.ShapeDtypeStruct((rows, 3 * blocks * devices), half),
            (SUB, incs),
            (clusters - 1, slots, edges),
        ],
        [tied(inc_path, first)[None, :], inc_edge[None, :], partner],
        scratch=[
            pltpu.VMEM((1, incs), jnp.int32),
            pltpu.VMEM((1, incs), jnp.int32),
            pltpu.SMEM((1, slots), jnp.int32),
            pltpu.SemaphoreType.DMA((3,)),
        ],
        pin=True,
    )

    limits_end, kept = 2 * blocks, 2 * blocks + SUB
    near_firsts = share(first, stages[:-1])
    groups = [p[k : k + kept + blocks] for p in near_firsts for k in range(0, p.shape[0], kept + blocks)]
    utilities = [p[kept:] for p in groups]
    firsts = [jnp.concatenate([groups[0][:kept], *[p[:limits_end] for p in groups[1:]]], axis=0)]
    inc = pl.pallas_call(
        cast_kernel,
        grid=(4,),
        in_specs=[pl.BlockSpec((incs // 4, width, edges), lambda k: (k, 0, 0))],
        out_specs=pl.BlockSpec((incs // 4, width, edges), lambda k: (k, 0, 0)),
        out_shape=jax.ShapeDtypeStruct(incidence.shape, half),
        compiler_params=pltpu.CompilerParams(vmem_limit_bytes=16 * 1024 * 1024),
        cost_estimate=pl.CostEstimate(flops=0, bytes_accessed=6 * incidence.size, transcendentals=0),
        name="cast",
    )(tied(incidence, firsts[-1]))
    firsts = [tied(firsts[0], onehot)]
    firsts = share(firsts, stages[-1:], bits - stages[-1])
    far_count, stride = 1 << stages[-1], devices >> stages[-1]
    own_same, other_same = kernel_call(
        lambda *refs: relate_kernel(far_count, blocks, incs, stride, *refs), "relate",
        [
            jax.ShapeDtypeStruct((far_count * rows, 3 * (incs + stride * blocks)), half),
            jax.ShapeDtypeStruct((far_count * rows, 3 * incs * (stride - 1)), half),
        ],
        [*firsts, *near_firsts],
    )

    others = clusters - 1
    flops = 2 * incs * width * edges * SUB
    load_shapes = [(rows, width), (locals_, edges), (slots, edges)]
    flows, load, out = kernel_call(
        lambda *refs: start_kernel(len(firsts), *refs), "first_load",
        [(rows, width), (locals_, edges), (3 * slots, edges)],
        [*firsts[1:], firsts[0], onehot, mask, inc, capacity, dual_start], flops=flops,
    )
    dual_shape, term_shape = (locals_, edges), (incs, width)
    (turned_inc,) = kernel_call(
        turn_kernel, "transpose", [jax.ShapeDtypeStruct((incs, edges, width), half)], [tied(inc, out)]
    )
    limit, duals, terms = kernel_call(
        lambda *refs: first_dual_kernel(others, unit, *refs), "first_duals",
        [dual_shape, dual_shape, term_shape],
        [*trade(out), choice, load, capacity, dual_start, mask, turned_inc], flops=flops,
    )
    for iteration in range(ITERS):
        near = share(terms, stages[:-1])
        if iteration == 0:
            (limits,) = kernel_call(
                lambda *refs: pick_kernel(len(firsts), blocks, *refs), "pick", [(rows, width)],
                [*firsts, onehot],
            )
        (part,) = kernel_call(
            part_kernel, "own_sums", [(far_count * rows, width)], [terms, *utilities, own_same]
        )
        if near[0].shape == terms.shape:
            near, skip = near[1:], 0
        else:
            skip = incs
        sums = kernel_call(
            lambda *refs: sum_kernel(len(near), skip, 1, *refs), "sums",
            [(rows, width)] * (far_count - 1), [*near, other_same, part],
        )
        (mine,) = kernel_call(
            lambda *refs: sum_kernel(len(near), skip, 0, *refs), "own_rows",
            [(rows, width)], [*near, other_same, tied(part, sums[0])],
        )
        far = [mine] + [
            lax.ppermute(x, "shard", [(i, i ^ (k * stride)) for i in range(devices)])
            for k, x in enumerate(sums, 1)
        ]
        flows, load, out = kernel_call(
            lambda *refs: flow_kernel(len(far), step_size, *refs), "flows", load_shapes,
            [far[2], far[3], far[1], far[0], flows, limits, mask, inc], flops=flops,
        )
        operands = [*trade(out), choice, load, limit, duals]
        if iteration < ITERS - 1:
            duals, terms = kernel_call(
                lambda *refs: dual_kernel(others, *refs), "duals", [dual_shape, term_shape],
                [*operands, mask, turned_inc], flops=flops,
            )
    (duals,) = kernel_call(
        lambda *refs: last_dual_kernel(others, *refs), "last_duals", [dual_shape], operands
    )
    return flows[incs:], duals


def solution(mesh):
    whole = P(("cluster", "shard"))
    wide = P(("cluster", "shard"), None)
    return jax.shard_map(
        body,
        mesh=mesh,
        in_specs=(
            wide, wide, wide, whole, P("cluster"), P(("cluster", "shard"), None, None),
            whole, whole, wide, wide, P("cluster", None),
        ),
        out_specs=(wide, wide),
        check_vma=False,
    )
```
